32 devices in a mesh: dp: 4 (over y, x), fsdp: 8 (over z, core).
Axes of the slice: x: 2, y: 2, z: 4, core: 2. Of those that a mesh axis runs over, the one named last changes fastest.
Arguments:
- tokens: bfloat16 [32, 1024, 768], P(('dp', 'fsdp')), may hold values from -6 to 6
- memory_init: float32 [10, 768], replicated, may hold values from -6 to 6
- chain_tokens: int32 [32], P(('dp', 'fsdp')), may hold values from 128 to 1024, as said below
- cotangent: bfloat16 [32, 1024, 768], P(('dp', 'fsdp')), may hold values from -6 to 6
- weights: float32 [9216, 768], P(('dp', 'fsdp'))
- weight_first: float32 [9216, 768], P(('dp', 'fsdp')), may hold values from -0.6 to 0.6
- weight_second: float32 [9216, 768], P(('dp', 'fsdp')), may hold values from 0.01 to 0.1
- vectors: float32 [12, 768], replicated
- vector_first: float32 [12, 768], replicated, may hold values from -0.6 to 0.6
- vector_second: float32 [12, 768], replicated, may hold values from 0.01 to 0.1
Outputs:
- output: float32 [32, 1024, 768], P(('dp', 'fsdp'))
- token_grad: float32 [32, 1024, 768], P(('dp', 'fsdp'))
- memory_grad: float32 [10, 768], replicated
- weight_grad: float32 [9216, 768], P(('dp', 'fsdp'))
- weight_step: float32 [9216, 768], P(('dp', 'fsdp'))
- new_weight_first: float32 [9216, 768], P(('dp', 'fsdp'))
- new_weight_second: float32 [9216, 768], P(('dp', 'fsdp'))
- vector_grad: float32 [12, 768], replicated
- vector_step: float32 [12, 768], replicated
- new_vector_first: float32 [12, 768], replicated
- new_vector_second: float32 [12, 768], replicated
The draws below stay inside these ranges and needn't reach their ends.
Inputs may be any that keep to these rules, and one draw needn't show every extreme that they name: `chain_tokens`: each chain's number of true tokens; one chain of every draw has 1024.
All inputs are finite; a program needn't handle non-finite values.
Results may differ from the reference program's by a relative error of at most 0.018.
The reference program's roundings to bfloat16 on the way count: a program that leaves them out, or rounds other values in their place, can miss the bound.
Values may be sent and summed in bfloat16 or wider, within the bound.
No kernel may reach another device: no remote copies, remote signals or barrier semaphores. Data moves between devices by JAX's collectives and lax.ppermute only.
A program may use at most 320 MiB of HBM per device.

```python
import math
import jax
import jax.numpy as jnp
from jax import lax

D = 768
HEADS = 12
HEAD_DIM = 64
FF = 3072
MEM = 10
SEG_LEN = 512
SEGS = 2
CHAINS = 32
W_ROWS = 9216
VEC_ROWS = 12


def draw_chain_tokens(key, part):
    key = jax.random.fold_in(key, 11)
    random_lengths = jax.random.randint(jax.random.fold_in(key, 1), (CHAINS,), SEG_LEN // 4, SEGS * SEG_LEN + 1, dtype=jnp.int32)
    longest = jax.random.randint(jax.random.fold_in(key, 2), (), 0, CHAINS, dtype=jnp.int32)
    chain_ids = jnp.arange(CHAINS, dtype=jnp.int32)
    return jnp.where(chain_ids == longest, SEGS * SEG_LEN, random_lengths).astype(jnp.int32)


def draw_weights(key, part):
    key = jax.random.fold_in(key, 12)
    row_ids = jnp.arange(W_ROWS, dtype=jnp.int32)[:, None]
    narrow = D ** (-0.5)
    scales = jnp.where(row_ids < 2 * D, 1.5 * narrow, jnp.where(row_ids < 3 * D, narrow, jnp.where(row_ids < 4 * D, 4.0 * narrow, jnp.where(row_ids < 4 * D + FF, narrow, FF ** (-0.5)))))
    values = jax.random.normal(key, (W_ROWS, D), jnp.float32)
    return (values * scales).astype(jnp.float32)


def draw_vectors(key, part):
    key = jax.random.fold_in(key, 13)
    row_ids = jnp.arange(VEC_ROWS, dtype=jnp.int32)[:, None]
    gains = 1.0 + 0.3 * jax.random.uniform(jax.random.fold_in(key, 1), (VEC_ROWS, D), jnp.float32, -1.0, 1.0)
    biases = 0.3 * jax.random.normal(jax.random.fold_in(key, 2), (VEC_ROWS, D), jnp.float32)
    is_gain = (row_ids == 3) | (row_ids == 6)
    return jnp.where(is_gain, gains, biases).astype(jnp.float32)


def steps_of(own_key, dims, cuts, low, high):
    gain = 1.0
    for position, parts in cuts:
        steps = jax.random.uniform(jax.random.fold_in(jax.random.fold_in(own_key, 6), position), (parts,), jnp.float32, low / len(cuts), high / len(cuts))
        gain = gain * jnp.repeat(jnp.exp(steps), dims[position] // parts).reshape((-1,) + (1,) * (len(dims) - 1 - position))
    return gain


def normal_values(rng, dims, width, reach, cuts=(), kind=jnp.bfloat16):
    values = width * jax.random.normal(rng, dims, jnp.float32)
    if cuts:
        values = values * steps_of(rng, dims, cuts, -0.22, 0.18)
    return jnp.clip(values, -reach, reach).astype(kind)


def setup_inputs(seed: int = 0) -> dict:
    key_list = jax.random.split(jax.random.key(seed), 11)
    return {
        "tokens": normal_values(key_list[0], (CHAINS, SEGS * SEG_LEN, D), 1.0, 6.0, ((0, 32),)),
        "memory_init": normal_values(key_list[1], (MEM, D), 1.0, 6.0, (), jnp.float32),
        "chain_tokens": draw_chain_tokens(jax.random.fold_in(key_list[10], 71), 0),
        "cotangent": normal_values(key_list[3], (CHAINS, SEGS * SEG_LEN, D), 1.0, 6.0, ((0, 32),)),
        "weights": draw_weights(jax.random.fold_in(key_list[10], 71), 0),
        "weight_first": normal_values(key_list[5], (W_ROWS, D), 0.1, 0.6, ((0, 32),), jnp.float32),
        "weight_second": jnp.clip(jnp.exp(math.log(0.1) - 2.3025851 * jax.random.uniform(key_list[6], (W_ROWS, D), jnp.float32) ** steps_of(key_list[6], (W_ROWS, D), ((0, 32),), -0.2, 0.2)), 0.01, 0.1),
        "vectors": draw_vectors(jax.random.fold_in(key_list[10], 71), 0),
        "vector_first": normal_values(key_list[8], (VEC_ROWS, D), 0.1, 0.6, (), jnp.float32),
        "vector_second": jnp.clip(jnp.exp(jax.random.uniform(key_list[9], (VEC_ROWS, D), jnp.float32, math.log(0.01), math.log(0.1))), 0.01, 0.1),
    }


@jax.custom_vjp
def low(v):
    return lax.optimization_barrier(v.astype(jnp.bfloat16)).astype(jnp.float32)

@jax.custom_vjp
def low_back(v):
    return v

def low_keep(v):
    return (low(v), None)

def low_pass(kept, grad):
    return (grad,)

def back_keep(v):
    return (v, None)

def back_low(kept, grad):
    return (low(grad),)
low.defvjp(low_keep, low_pass)
low_back.defvjp(back_keep, back_low)
eps_norm = 1e-12
beta_one = 0.9
beta_two = 0.95
decay_rate = 0.1
adam_eps = 1e-08
adam_step = 10

def matmul(form, left, right):
    return jnp.einsum(form, left, right, precision=lax.Precision.HIGHEST)

def layer_norm(values, gain_row, shift_row):
    centred = values - lax.optimization_barrier(jnp.mean(values, axis=-1, keepdims=True))
    inverse = lax.rsqrt(lax.optimization_barrier(jnp.mean(centred * centred, axis=-1, keepdims=True)) + eps_norm)
    return centred * inverse * gain_row + shift_row

def layer_segment(inputs, valid_keys, weights_all, vectors_all):
    chains = inputs.shape[0]
    row_count = inputs.shape[1]
    split_shape = (chains, row_count, HEADS, HEAD_DIM)
    w_query = weights_all[0:D]
    w_key = weights_all[D:2 * D]
    w_value = weights_all[2 * D:3 * D]
    w_out = weights_all[3 * D:4 * D]
    w_up = weights_all[4 * D:4 * D + FF]
    w_down = weights_all[4 * D + FF:]
    lowered = low(inputs)
    queries = low(low_back(matmul('cld,de->cle', lowered, w_query) + vectors_all[0])).reshape(split_shape)
    key_rows = low(low_back(matmul('cld,de->cle', lowered, w_key))).reshape(split_shape)
    value_rows = low(low_back(matmul('cld,de->cle', lowered, w_value) + vectors_all[1])).reshape(split_shape)
    scores = matmul('clhe,cmhe->chlm', queries, key_rows) * HEAD_DIM ** (-0.5)
    scores = low_back(jnp.where(valid_keys[:, None, None, :], scores, -1e+30))
    soft_low = low(jax.nn.softmax(scores, axis=-1))
    attended = matmul('chlm,cmhe->clhe', soft_low, value_rows).reshape(chains, row_count, D)
    attended = low(low_back(attended))
    branch = low_back(matmul('cld,de->cle', attended, w_out) + vectors_all[2])
    after_attention = layer_norm(inputs + branch, vectors_all[3], vectors_all[4])
    up_projection = low_back(matmul('cld,fd->clf', low(after_attention), w_up) + vectors_all[8:].reshape(-1))
    activated = low(jax.nn.gelu(up_projection, approximate=False))
    feed_output = low_back(matmul('clf,fd->cld', activated, w_down) + vectors_all[5])
    return layer_norm(after_attention + feed_output, vectors_all[6], vectors_all[7])

def chains_forward(tokens_group, lengths, memory_start, weights_all, vectors_all):
    chains = tokens_group.shape[0]
    memory_state = jnp.broadcast_to(memory_start, (chains, MEM, D))
    positions = jnp.arange(SEG_LEN, dtype=jnp.int32)
    always = jnp.ones((chains, MEM), dtype=jnp.bool_)
    output_rows = []
    for segment in range(SEGS):
        offset = segment * SEG_LEN
        token_live = positions[None, :] + offset < lengths[:, None]
        segment_real = offset < lengths
        valid_keys = jnp.concatenate([always, token_live, always], axis=1)
        inputs = jnp.concatenate([memory_state, tokens_group[:, offset:offset + SEG_LEN], memory_state], axis=1)
        result = layer_segment(inputs, valid_keys, weights_all, vectors_all)
        output_rows.append(jnp.where(token_live[..., None], result[:, MEM:MEM + SEG_LEN], 0.0))
        written = result[:, MEM + SEG_LEN:]
        memory_state = jnp.where(segment_real[:, None, None], written, memory_state)
    return jnp.concatenate(output_rows, axis=1)

def adam_update(parameter, gradient, moment_one, moment_two, decay_factor):
    new_one = beta_one * moment_one + (1.0 - beta_one) * gradient
    new_two = beta_two * moment_two + (1.0 - beta_two) * gradient * gradient
    corrected_one = new_one / (1.0 - beta_one ** adam_step)
    corrected_two = new_two / (1.0 - beta_two ** adam_step)
    update = corrected_one / (jnp.sqrt(corrected_two) + adam_eps) + decay_factor * parameter
    return (update, new_one, new_two)

def reference(tokens, memory_init, chain_tokens, cotangent, weights, weight_first, weight_second, vectors, vector_first, vector_second):
    group_size = math.gcd(CHAINS, max(1, 4096 // (SEGS * SEG_LEN)))
    group_count = CHAINS // group_size
    chain_length = SEGS * SEG_LEN
    grouped_lengths = chain_tokens.reshape(group_count, group_size)

    def whole_forward(tokens_float, memory_float, weights_float, vectors_float):
        weights_low = low(weights_float)

        def run_group(pieces):
            return jax.checkpoint(chains_forward)(pieces[0], pieces[1], memory_float, weights_low, vectors_float)
        results = lax.map(run_group, (tokens_float.reshape(group_count, group_size, chain_length, D), grouped_lengths))
        return results.reshape(CHAINS, chain_length, D)
    result, pullback = jax.vjp(whole_forward, tokens.astype(jnp.float32), memory_init, weights, vectors)
    token_grad, memory_sum, weight_sum, vector_sum = pullback(cotangent.astype(jnp.float32))
    grad_scale = float(CHAINS * SEGS * SEG_LEN) ** (-0.5)
    weight_grad = weight_sum * grad_scale
    vector_grad = vector_sum * grad_scale
    memory_grad = memory_sum * grad_scale
    weight_step, new_weight_first, new_weight_second = adam_update(weights, weight_grad, weight_first, weight_second, decay_rate)
    vector_step, new_vector_first, new_vector_second = adam_update(vectors, vector_grad, vector_first, vector_second, 0.0)
    return (result, token_grad, memory_grad, weight_grad, weight_step, new_weight_first, new_weight_second, vector_grad, vector_step, new_vector_first, new_vector_second)
```

```python
import functools

import jax
import jax.numpy as jnp
from jax import lax
from jax.experimental import pallas as pl
from jax.experimental.pallas import tpu as pltpu
from jax.sharding import PartitionSpec as P

D = 768
HEADS = 12
HEAD = 64
FF = 3072
MEM = 10
SEG_LEN = 512
SEGS = 2
PADM = 16
ROWS = SEG_LEN + 2 * PADM
ROWS_LANES = -(-ROWS // 128) * 128
COLS = 256
STEPS = D // COLS
CHUNKS = FF // D

eps_norm = 1e-12
beta_one = 0.9
beta_two = 0.95
decay_rate = 0.1
adam_eps = 1e-08
adam_step = 10
neg_large = -1e30
LOG2E = 1.4426950408889634
SCORE2 = HEAD ** (-0.5) * LOG2E
ROOT = HEAD ** (-0.5)
f32 = jnp.float32
bf16 = jnp.bfloat16
VMEM_BYTES = 56 * 1024 * 1024


def dot_nn(left, right):
    return lax.dot_general(left, right, (((1,), (0,)), ((), ())), preferred_element_type=f32)


def dot_nt(left, right):
    return lax.dot_general(left, right, (((1,), (1,)), ((), ())), preferred_element_type=f32)


def dot_tn(left, right):
    return lax.dot_general(left, right, (((0,), (0,)), ((), ())), preferred_element_type=f32)


def valid_positions(shape, axis, live):
    at = lax.broadcasted_iota(jnp.int32, shape, axis)
    read = (at >= SEG_LEN) & (at < SEG_LEN + MEM)
    write = (at >= SEG_LEN + PADM) & (at < SEG_LEN + PADM + MEM)
    return (at < live) | read | write


def mask_half(values, half):
    lane = lax.broadcasted_iota(jnp.int32, values.shape, 1)
    keep = (lane < HEAD) if half == 0 else (lane >= HEAD)
    return jnp.where(keep, values, jnp.zeros_like(values))


def norm_rows(values):
    centred = values - jnp.mean(values, axis=-1, keepdims=True)
    inverse = lax.rsqrt(jnp.mean(centred * centred, axis=-1, keepdims=True) + eps_norm)
    return centred * inverse, inverse


def norm_back(gradient, normed, inverse, gain_row):
    scaled = gradient * gain_row
    centred = scaled - jnp.mean(scaled, axis=-1, keepdims=True)
    return inverse * (centred - normed * jnp.mean(scaled * normed, axis=-1, keepdims=True))


def gelu_parts(z):
    gauss = jnp.exp2(z * z * (-0.5 * LOG2E))
    base = 1.0 + jnp.abs(z) * (0.3275911 * 0.7071067811865476)
    t = pl.reciprocal(base, approx=True)
    t = t * (2.0 - base * t)
    poly = 0.5 * 1.061405429
    poly = poly * t + 0.5 * -1.453152027
    poly = poly * t + 0.5 * 1.421413741
    poly = poly * t + 0.5 * -0.284496736
    poly = poly * t + 0.5 * 0.254829592
    tail = poly * t * gauss
    phi = jnp.where(z >= 0.0, 1.0 - tail, tail)
    return z * phi, phi + z * gauss * 0.3989422804014327


def attn_fwd_kernel(
    live_ref, tok_ref, mem_ref, wq_ref, wk_ref, wv_ref, vec_ref,
    x_ref, q_ref, k_ref, v_ref, lse_ref, a_ref, lse_acc,
):
    step = pl.program_id(0)
    live = live_ref[0]

    @pl.when(step == 0)
    def _():
        x_ref[0:SEG_LEN] = tok_ref[...]
        low = mem_ref[...].astype(bf16)
        x_ref[SEG_LEN:SEG_LEN + PADM] = low
        x_ref[SEG_LEN + PADM:ROWS] = low
        lse_acc[...] = jnp.zeros_like(lse_acc)

    x = x_ref[...]
    q = (dot_nn(x, wq_ref[...]) + vec_ref[0:1]).astype(bf16)
    k = dot_nn(x, wk_ref[...]).astype(bf16)
    v = (dot_nn(x, wv_ref[...]) + vec_ref[1:2]).astype(bf16)
    q_ref[...] = q
    k_ref[...] = k
    v_ref[...] = v
    valid = valid_positions((1, ROWS), 1, live)
    lane = lax.broadcasted_iota(jnp.int32, (1, 128), 1)
    lse_all = lse_acc[0:ROWS]
    for pair in range(COLS // 128):
        cols = slice(128 * pair, 128 * pair + 128)
        qp, kp, vp = q[:, cols], k[:, cols], v[:, cols]
        total = None
        for half in range(2):
            s = dot_nt(qp, mask_half(kp, half))
            s = jnp.where(valid, s, neg_large)
            top = jnp.max(s, axis=1, keepdims=True)
            e = jnp.exp2((s - top) * SCORE2)
            amount = jnp.sum(e, axis=1, keepdims=True)
            p = (e * (1.0 / amount)).astype(bf16)
            lse = top * SCORE2 + jnp.log(amount) * LOG2E
            head = step * (COLS // HEAD) + 2 * pair + half
            lse_all = jnp.where(lane == head, lse, lse_all)
            part = dot_nn(p, mask_half(vp, half))
            total = part if total is None else total + part
        a_ref[:, cols] = total.astype(bf16)
    lse_acc[0:ROWS] = lse_all

    @pl.when(step == STEPS - 1)
    def _():
        lse_ref[...] = lse_acc[...].T[0:16]


def ffn_fwd_kernel(
    live_ref, tok_ref, mem_ref, a_ref, wo_ref, wu_ref, wd_ref, vec_ref,
    n1_ref, i1_ref, h1b_ref, g_ref, slope_ref, n2_ref, i2_ref, out_ref, next_ref,
    h1, acc,
):
    step = pl.program_id(0)
    live = live_ref[0]

    @pl.when(step == 0)
    def _():
        branch = dot_nn(a_ref[...], wo_ref[...]) + vec_ref[2:3]
        mem = mem_ref[...]
        u = jnp.concatenate([tok_ref[...].astype(f32), mem, mem], axis=0)
        normed, inverse = norm_rows(u + branch)
        n1_ref[...] = normed
        i1_ref[...] = inverse
        full = normed * vec_ref[3:4] + vec_ref[4:5]
        h1[...] = full
        h1b_ref[...] = full.astype(bf16)
        acc[...] = full + vec_ref[5:6]

    z = dot_nt(h1b_ref[...], wu_ref[...]) + vec_ref[pl.ds(8 + step, 1), :]
    g, slope = gelu_parts(z)
    g = g.astype(bf16)
    g_ref[...] = g
    slope_ref[...] = slope
    acc[...] += dot_nn(g, wd_ref[...])

    @pl.when(step == CHUNKS - 1)
    def _():
        normed, inverse = norm_rows(acc[...])
        n2_ref[...] = normed
        i2_ref[...] = inverse
        y = normed * vec_ref[6:7] + vec_ref[7:8]
        row = lax.broadcasted_iota(jnp.int32, (SEG_LEN, 1), 0)
        out_ref[...] = jnp.where(row < live, y[0:SEG_LEN], 0.0)
        next_ref[...] = jnp.where(live > 0, y[SEG_LEN + PADM:ROWS], mem_ref[...])


def ffn_bwd_kernel(
    live_ref, cot_ref, dmem_ref, n1_ref, i1_ref, n2_ref, i2_ref, slope_ref, wo_ref, wu_ref, wd_ref, vec_ref,
    dfb_ref, dzb_ref, dob_ref, dr1_ref, da_ref, sums_ref,
    acc,
):
    step = pl.program_id(0)
    live = live_ref[0]

    @pl.when(step == 0)
    def _():
        row = lax.broadcasted_iota(jnp.int32, (SEG_LEN, 1), 0)
        token = jnp.where(row < live, cot_ref[...].astype(f32), 0.0)
        write = jnp.where(live > 0, dmem_ref[...], 0.0)
        dy = jnp.concatenate([token, jnp.zeros((PADM, D), f32), write], axis=0)
        normed = n2_ref[...]
        sums_ref[...] = jnp.zeros_like(sums_ref)
        sums_ref[6:7] = jnp.sum(dy * normed, axis=0, keepdims=True)
        sums_ref[7:8] = jnp.sum(dy, axis=0, keepdims=True)
        back = norm_back(dy, normed, i2_ref[...], vec_ref[6:7])
        low = back.astype(bf16)
        dfb_ref[...] = low
        sums_ref[5:6] = jnp.sum(low.astype(f32), axis=0, keepdims=True)
        acc[...] = back

    dz = (dot_nt(dfb_ref[...], wd_ref[...]) * slope_ref[...]).astype(bf16)
    dzb_ref[...] = dz
    sums_ref[pl.ds(8 + step, 1), :] = jnp.sum(dz.astype(f32), axis=0, keepdims=True)
    acc[...] += dot_nn(dz, wu_ref[...])

    @pl.when(step == CHUNKS - 1)
    def _():
        dh = acc[...]
        normed = n1_ref[...]
        sums_ref[3:4] = jnp.sum(dh * normed, axis=0, keepdims=True)
        sums_ref[4:5] = jnp.sum(dh, axis=0, keepdims=True)
        back = norm_back(dh, normed, i1_ref[...], vec_ref[3:4])
        dr1_ref[...] = back
        low = back.astype(bf16)
        dob_ref[...] = low
        sums_ref[2:3] = jnp.sum(low.astype(f32), axis=0, keepdims=True)
        da_ref[...] = dot_nt(low, wo_ref[...]).astype(bf16)


def attn_bwd_kernel(
    live_ref, q_ref, k_ref, v_ref, da_ref, lse_ref, dr1_ref, wq_ref, wk_ref, wv_ref,
    dq_ref, dk_ref, dv_ref, sums_ref, du_ref,
):
    step = pl.program_id(0)
    live = live_ref[0]

    @pl.when(step == 0)
    def _():
        du_ref[...] = dr1_ref[...]

    valid = valid_positions((ROWS, 1), 0, live)
    for pair in range(COLS // 128):
        cols = slice(128 * pair, 128 * pair + 128)
        qp, kp, vp, dap = q_ref[:, cols], k_ref[:, cols], v_ref[:, cols], da_ref[:, cols]
        dq = dk = dv = None
        for half in range(2):
            head = step * (COLS // HEAD) + 2 * pair + half
            kh, vh, qh, dah = (mask_half(t, half) for t in (kp, vp, qp, dap))
            s = dot_nt(kh, qp)
            s = jnp.where(valid, s, neg_large)
            p = jnp.exp2(s * SCORE2 - lse_ref[pl.ds(head, 1), 0:ROWS])
            dp = dot_nt(vh, dap)
            inner = jnp.sum(p * dp, axis=0, keepdims=True)
            ds = (p * (dp - inner)).astype(bf16)
            parts = (dot_tn(ds, kh), dot_nn(ds, qh), dot_nn(p.astype(bf16), dah))
            if dq is None:
                dq, dk, dv = parts
            else:
                dq, dk, dv = dq + parts[0], dk + parts[1], dv + parts[2]
        dq_ref[:, cols] = (dq * ROOT).astype(bf16)
        dk_ref[:, cols] = (dk * ROOT).astype(bf16)
        dv_ref[:, cols] = dv.astype(bf16)
    dq, dk, dv = dq_ref[...], dk_ref[...], dv_ref[...]
    sums_ref[0:1] = jnp.sum(dq.astype(f32), axis=0, keepdims=True)
    sums_ref[1:2] = jnp.sum(dv.astype(f32), axis=0, keepdims=True)
    du_ref[...] += dot_nt(dq, wq_ref[...]) + dot_nt(dk, wk_ref[...]) + dot_nt(dv, wv_ref[...])


def grad_ffn_kernel(dz0_ref, dz1_ref, g0_ref, g1_ref, h0_ref, h1_ref, df0_ref, df1_ref, out_ref):
    step = pl.program_id(0)

    @pl.when(step < CHUNKS)
    def _():
        out_ref[...] = (dot_tn(dz0_ref[...], h0_ref[...]) + dot_tn(dz1_ref[...], h1_ref[...])).astype(bf16)

    @pl.when(step >= CHUNKS)
    def _():
        out_ref[...] = (dot_tn(g0_ref[...], df0_ref[...]) + dot_tn(g1_ref[...], df1_ref[...])).astype(bf16)


def grad_attn_kernel(x0_ref, x1_ref, a0_ref, a1_ref, r0_ref, r1_ref, k0_ref, k1_ref, v0_ref, v1_ref, o0_ref, o1_ref, out_ref):
    step = pl.program_id(0)
    for index, (left0, left1, right0, right1) in enumerate((
        (x0_ref, x1_ref, r0_ref, r1_ref), (x0_ref, x1_ref, k0_ref, k1_ref),
        (x0_ref, x1_ref, v0_ref, v1_ref), (a0_ref, a1_ref, o0_ref, o1_ref),
    )):
        @pl.when(step == index)
        def _(left0=left0, left1=left1, right0=right0, right1=right1):
            out_ref[...] = (dot_tn(left0[...], right0[...]) + dot_tn(left1[...], right1[...])).astype(bf16)


def spec(shape, index):
    return pl.BlockSpec(shape, index)


def whole(shape):
    return pl.BlockSpec(shape, lambda j: (0,) * len(shape))


SCALAR = pl.BlockSpec(memory_space=pltpu.SMEM)


def shape_of(shape, dtype):
    return jax.ShapeDtypeStruct(shape, dtype)


def params():
    return pltpu.CompilerParams(dimension_semantics=("arbitrary",), vmem_limit_bytes=VMEM_BYTES)


def cost(flops, moved):
    return pl.CostEstimate(flops=int(flops), bytes_accessed=int(moved), transcendentals=0)


def attn_fwd(segment, live, tokens, mem, weights, vectors):
    block = spec((ROWS, COLS), lambda j: (0, j))
    return pl.pallas_call(
        attn_fwd_kernel,
        grid=(STEPS,),
        in_specs=[
            SCALAR, spec((SEG_LEN, D), lambda j: (segment, 0)), whole((PADM, D)),
            spec((D, COLS), lambda j: (0, j)), spec((D, COLS), lambda j: (1, j)), spec((D, COLS), lambda j: (2, j)),
            spec((12, COLS), lambda j: (0, j)),
        ],
        out_specs=[whole((ROWS, D)), block, block, block, whole((16, ROWS_LANES)), block],
        out_shape=[shape_of((ROWS, D), bf16)] * 4 + [shape_of((16, ROWS_LANES), f32), shape_of((ROWS, D), bf16)],
        scratch_shapes=[pltpu.VMEM((ROWS_LANES, 128), f32)],
        compiler_params=params(),
        name="attn_fwd",
        cost_estimate=cost(5e9, 8e6),
    )(live, tokens, mem, weights, weights, weights, vectors)


def ffn_fwd(segment, live, tokens, mem, attended, weights, vectors):
    full = whole((ROWS, D))
    chunk = spec((ROWS, D), lambda j: (0, j))
    col = whole((ROWS, 1))
    return pl.pallas_call(
        ffn_fwd_kernel,
        grid=(CHUNKS,),
        in_specs=[
            SCALAR, spec((SEG_LEN, D), lambda j: (segment, 0)), whole((PADM, D)), full,
            spec((D, D), lambda j: (3, 0)), spec((D, D), lambda j: (4 + j, 0)), spec((D, D), lambda j: (8 + j, 0)),
            whole((12, D)),
        ],
        out_specs=[full, col, full, chunk, chunk, full, col, whole((SEG_LEN, D)), whole((PADM, D))],
        out_shape=[
            shape_of((ROWS, D), f32), shape_of((ROWS, 1), f32), shape_of((ROWS, D), bf16), shape_of((ROWS, FF), bf16),
            shape_of((ROWS, FF), f32), shape_of((ROWS, D), f32), shape_of((ROWS, 1), f32),
            shape_of((SEG_LEN, D), f32), shape_of((PADM, D), f32),
        ],
        scratch_shapes=[pltpu.VMEM((ROWS, D), f32)] * 2,
        compiler_params=params(),
        name="ffn_fwd",
        cost_estimate=cost(6e9, 25e6),
    )(live, tokens, mem, attended, weights, weights, weights, vectors)


def ffn_bwd(segment, live, cotangent, dmem, saved, weights, vectors):
    n1, i1, h1b, g, slope, n2, i2 = saved
    full = whole((ROWS, D))
    chunk = spec((ROWS, D), lambda j: (0, j))
    col = whole((ROWS, 1))
    return pl.pallas_call(
        ffn_bwd_kernel,
        grid=(CHUNKS,),
        in_specs=[
            SCALAR, spec((SEG_LEN, D), lambda j: (segment, 0)), whole((PADM, D)), full, col, full, col, chunk,
            spec((D, D), lambda j: (3, 0)), spec((D, D), lambda j: (4 + j, 0)), spec((D, D), lambda j: (8 + j, 0)),
            whole((12, D)),
        ],
        out_specs=[full, chunk, full, full, full, whole((12, D))],
        out_shape=[
            shape_of((ROWS, D), bf16), shape_of((ROWS, FF), bf16), shape_of((ROWS, D), bf16),
            shape_of((ROWS, D), f32), shape_of((ROWS, D), bf16), shape_of((12, D), f32),
        ],
        scratch_shapes=[pltpu.VMEM((ROWS, D), f32)],
        compiler_params=params(),
        name="ffn_bwd",
        cost_estimate=cost(6e9, 25e6),
    )(live, cotangent, dmem, n1, i1, n2, i2, slope, weights, weights, weights, vectors)


def attn_bwd(live, q, k, v, da, lse, dr1, weights):
    block = spec((ROWS, COLS), lambda j: (0, j))
    return pl.pallas_call(
        attn_bwd_kernel,
        grid=(STEPS,),
        in_specs=[
            SCALAR, block, block, block, block, whole((16, ROWS_LANES)), whole((ROWS, D)),
            spec((D, COLS), lambda j: (0, j)), spec((D, COLS), lambda j: (1, j)), spec((D, COLS), lambda j: (2, j)),
        ],
        out_specs=[block, block, block, spec((8, COLS), lambda j: (0, j)), whole((ROWS, D))],
        out_shape=[shape_of((ROWS, D), bf16)] * 3 + [
            shape_of((8, D), f32), shape_of((ROWS, D), f32)],
        compiler_params=params(),
        name="attn_bwd",
        cost_estimate=cost(10e9, 10e6),
    )(live, q, k, v, da, lse, dr1, weights, weights, weights)


def grad_ffn(dz, g, h, df):
    up = spec((ROWS, D), lambda j: (0, jnp.minimum(j, CHUNKS - 1)))
    down = spec((ROWS, D), lambda j: (0, jnp.maximum(j - CHUNKS, 0)))
    full = whole((ROWS, D))
    return pl.pallas_call(
        grad_ffn_kernel,
        grid=(2 * CHUNKS,),
        in_specs=[up, up, down, down, full, full, full, full],
        out_specs=spec((D, D), lambda j: (j, 0)),
        out_shape=shape_of((2 * FF, D), bf16),
        compiler_params=params(),
        name="grad_ffn",
        cost_estimate=cost(10e9, 25e6),
    )(*dz, *g, *h, *df)


def grad_attn(x, a, dq, dk, dv, do):
    full = whole((ROWS, D))
    return pl.pallas_call(
        grad_attn_kernel,
        grid=(4,),
        in_specs=[full] * 12,
        out_specs=spec((D, D), lambda j: (j, 0)),
        out_shape=shape_of((4 * D, D), bf16),
        compiler_params=params(),
        name="grad_attn",
        cost_estimate=cost(5e9, 15e6),
    )(*x, *a, *dq, *dk, *dv, *do)


def adam_update(parameter, gradient, moment_one, moment_two, decay_factor):
    new_one = beta_one * moment_one + (1.0 - beta_one) * gradient
    new_two = beta_two * moment_two + (1.0 - beta_two) * gradient * gradient
    corrected_one = new_one / (1.0 - beta_one**adam_step)
    corrected_two = new_two / (1.0 - beta_two**adam_step)
    update = corrected_one / (jnp.sqrt(corrected_two) + adam_eps) + decay_factor * parameter
    return (update, new_one, new_two)


def local_grads(tokens, memory_init, chain_tokens, cotangent, weights, vectors):
    mem = jnp.pad(memory_init, ((0, PADM - MEM), (0, 0)))
    lives = [jnp.clip(chain_tokens - s * SEG_LEN, 0, SEG_LEN) for s in range(SEGS)]
    kept = []
    outputs = []
    for s in range(SEGS):
        x, q, k, v, lse, a = attn_fwd(s, lives[s], tokens, mem, weights, vectors)
        *saved, out, mem = ffn_fwd(s, lives[s], tokens, mem, a, weights, vectors)
        kept.append((x, q, k, v, lse, a, saved))
        outputs.append(out)
    dmem = jnp.zeros((PADM, D), f32)
    back = [None] * SEGS
    token_grads = [None] * SEGS
    for s in reversed(range(SEGS)):
        x, q, k, v, lse, a, saved = kept[s]
        dfb, dzb, dob, dr1, da, sums = ffn_bwd(s, lives[s], cotangent, dmem, saved, weights, vectors)
        dq, dk, dv, sums_qv, du = attn_bwd(lives[s], q, k, v, da, lse, dr1, weights)
        token_grads[s] = du[:SEG_LEN]
        dmem = du[SEG_LEN:SEG_LEN + PADM] + du[SEG_LEN + PADM:] + jnp.where(lives[s] > 0, 0.0, dmem)
        back[s] = (dfb, dzb, dob, dq, dk, dv, sums, sums_qv)
    pick = lambda items, i: [item[i] for item in items]
    wide = grad_ffn(pick(back, 1), [k_[6][3] for k_ in kept], [k_[6][2] for k_ in kept], pick(back, 0))
    square = grad_attn(pick(kept, 0), pick(kept, 5), pick(back, 3), pick(back, 4), pick(back, 5), pick(back, 2))
    sums = sum(pick(back, 6))
    sums_qv = sum(pick(back, 7))
    vector_total = jnp.concatenate([sums_qv[0:2], sums[2:]], axis=0)
    return (jnp.concatenate(outputs, 0), jnp.concatenate(token_grads, 0), dmem[:MEM], square, wide, vector_total)


def shards(
    tokens, memory_init, chain_tokens, cotangent, weights, weight_first, weight_second,
    vectors, vector_first, vector_second,
):
    axes = ("dp", "fsdp")
    total_chains = tokens.shape[0] * lax.axis_size(axes)
    grad_scale = float(total_chains * SEGS * SEG_LEN) ** (-0.5)
    gathered = lax.all_gather(weights.astype(bf16), axes, axis=0, tiled=True)
    output, token_grad, memory_local, square, wide, vector_total = local_grads(
        tokens[0], memory_init, chain_tokens, cotangent[0], gathered, vectors)
    matrix_total = jnp.concatenate([square, wide], axis=0)
    weight_sum = lax.psum_scatter(matrix_total, axes, scatter_dimension=0, tiled=True).astype(f32)
    vector_sum, memory_sum = lax.psum((vector_total, memory_local), axes)
    weight_grad = weight_sum * grad_scale
    vector_grad = vector_sum * grad_scale
    memory_grad = memory_sum * grad_scale
    weight_step, new_weight_first, new_weight_second = adam_update(
        weights, weight_grad, weight_first, weight_second, decay_rate)
    vector_step, new_vector_first, new_vector_second = adam_update(
        vectors, vector_grad, vector_first, vector_second, 0.0)
    return (
        output[None], token_grad[None], memory_grad, weight_grad, weight_step, new_weight_first, new_weight_second,
        vector_grad, vector_step, new_vector_first, new_vector_second,
    )


def solution(mesh):
    both = ("dp", "fsdp")
    chain = P(both, None, None)
    rows = P(both, None)
    return jax.shard_map(
        shards,
        mesh=mesh,
        in_specs=(chain, P(), P(both), chain, rows, rows, rows, P(), P(), P()),
        out_specs=(chain, chain, P(), rows, rows, rows, rows, P(), P(), P(), P()),
        check_vma=False,
    )
```

```python
import functools

import jax
import jax.numpy as jnp
from jax import lax
from jax.experimental import pallas as pl
from jax.experimental.pallas import tpu as pltpu
from jax.sharding import PartitionSpec as P

D = 768
HEADS = 12
HEAD = 64
FF = 3072
MEM = 10
SEG_LEN = 512
SEGS = 2
PADM = 16
ROWS = SEG_LEN + 2 * PADM
ROWS_LANES = -(-ROWS // 128) * 128
COLS = 256
STEPS = D // COLS
CHUNKS = FF // D

eps_norm = 1e-12
beta_one = 0.9
beta_two = 0.95
decay_rate = 0.1
adam_eps = 1e-08
adam_step = 10
neg_large = -1e30
LOG2E = 1.4426950408889634
SCORE2 = HEAD ** (-0.5) * LOG2E
ROOT = HEAD ** (-0.5)
f32 = jnp.float32
bf16 = jnp.bfloat16
VMEM_BYTES = 56 * 1024 * 1024


def dot_nn(left, right):
    return lax.dot_general(left, right, (((1,), (0,)), ((), ())), preferred_element_type=f32)


def dot_nt(left, right):
    return lax.dot_general(left, right, (((1,), (1,)), ((), ())), preferred_element_type=f32)


def dot_tn(left, right):
    return lax.dot_general(left, right, (((0,), (0,)), ((), ())), preferred_element_type=f32)


def valid_positions(shape, axis, live):
    at = lax.broadcasted_iota(jnp.int32, shape, axis)
    read = (at >= SEG_LEN) & (at < SEG_LEN + MEM)
    write = (at >= SEG_LEN + PADM) & (at < SEG_LEN + PADM + MEM)
    return (at < live) | read | write


def mask_half(values, half):
    lane = lax.broadcasted_iota(jnp.int32, values.shape, 1)
    keep = (lane < HEAD) if half == 0 else (lane >= HEAD)
    return jnp.where(keep, values, jnp.zeros_like(values))


def norm_rows(values):
    centred = values - jnp.mean(values, axis=-1, keepdims=True)
    inverse = lax.rsqrt(jnp.mean(centred * centred, axis=-1, keepdims=True) + eps_norm)
    return centred * inverse, inverse


def norm_back(gradient, normed, inverse, gain_row):
    scaled = gradient * gain_row
    centred = scaled - jnp.mean(scaled, axis=-1, keepdims=True)
    return inverse * (centred - normed * jnp.mean(scaled * normed, axis=-1, keepdims=True))


def gelu_parts(z):
    gauss = jnp.exp2(z * z * (-0.5 * LOG2E))
    base = 1.0 + jnp.abs(z) * (0.3275911 * 0.7071067811865476)
    t = pl.reciprocal(base, approx=True)
    t = t * (2.0 - base * t)
    poly = 0.5 * 1.061405429
    poly = poly * t + 0.5 * -1.453152027
    poly = poly * t + 0.5 * 1.421413741
    poly = poly * t + 0.5 * -0.284496736
    poly = poly * t + 0.5 * 0.254829592
    tail = poly * t * gauss
    phi = jnp.where(z >= 0.0, 1.0 - tail, tail)
    return z * phi, phi + z * gauss * 0.3989422804014327


def attn_fwd_kernel(
    live_ref, tok_ref, mem_ref, wq_ref, wk_ref, wv_ref, vec_ref,
    x_ref, q_ref, k_ref, v_ref, lse_ref, a_ref, lse_acc,
):
    step = pl.program_id(0)
    live = live_ref[0]

    @pl.when(step == 0)
    def _():
        x_ref[0:SEG_LEN] = tok_ref[...]
        low = mem_ref[...].astype(bf16)
        x_ref[SEG_LEN:SEG_LEN + PADM] = low
        x_ref[SEG_LEN + PADM:ROWS] = low
        lse_acc[...] = jnp.zeros_like(lse_acc)

    x = x_ref[...]
    q = (dot_nn(x, wq_ref[...]) + vec_ref[0:1]).astype(bf16)
    k = dot_nn(x, wk_ref[...]).astype(bf16)
    v = (dot_nn(x, wv_ref[...]) + vec_ref[1:2]).astype(bf16)
    q_ref[...] = q
    k_ref[...] = k
    v_ref[...] = v
    valid = valid_positions((1, ROWS), 1, live)
    lane = lax.broadcasted_iota(jnp.int32, (1, 128), 1)
    lse_all = lse_acc[0:ROWS]
    for pair in range(COLS // 128):
        cols = slice(128 * pair, 128 * pair + 128)
        qp, kp, vp = q[:, cols], k[:, cols], v[:, cols]
        total = None
        for half in range(2):
            s = dot_nt(qp, mask_half(kp, half))
            s = jnp.where(valid, s, neg_large)
            top = jnp.max(s, axis=1, keepdims=True)
            e = jnp.exp2((s - top) * SCORE2)
            amount = jnp.sum(e, axis=1, keepdims=True)
            p = (e * (1.0 / amount)).astype(bf16)
            lse = top * SCORE2 + jnp.log(amount) * LOG2E
            head = step * (COLS // HEAD) + 2 * pair + half
            lse_all = jnp.where(lane == head, lse, lse_all)
            part = dot_nn(p, mask_half(vp, half))
            total = part if total is None else total + part
        a_ref[:, cols] = total.astype(bf16)
    lse_acc[0:ROWS] = lse_all

    @pl.when(step == STEPS - 1)
    def _():
        lse_ref[...] = lse_acc[...].T[0:16]


def ffn_fwd_kernel(
    live_ref, tok_ref, mem_ref, a_ref, wo_ref, wu_ref, wd_ref, vec_ref,
    n1_ref, i1_ref, h1b_ref, g_ref, slope_ref, n2_ref, i2_ref, out_ref, next_ref,
    h1, acc,
):
    step = pl.program_id(0)
    live = live_ref[0]

    @pl.when(step == 0)
    def _():
        branch = dot_nn(a_ref[...], wo_ref[...]) + vec_ref[2:3]
        mem = mem_ref[...]
        u = jnp.concatenate([tok_ref[...].astype(f32), mem, mem], axis=0)
        normed, inverse = norm_rows(u + branch)
        n1_ref[...] = normed
        i1_ref[...] = inverse
        full = normed * vec_ref[3:4] + vec_ref[4:5]
        h1[...] = full
        h1b_ref[...] = full.astype(bf16)
        acc[...] = full + vec_ref[5:6]

    z = dot_nt(h1b_ref[...], wu_ref[...]) + vec_ref[pl.ds(8 + step, 1), :]
    g, slope = gelu_parts(z)
    g = g.astype(bf16)
    g_ref[...] = g
    slope_ref[...] = slope
    acc[...] += dot_nn(g, wd_ref[...])

    @pl.when(step == CHUNKS - 1)
    def _():
        normed, inverse = norm_rows(acc[...])
        n2_ref[...] = normed
        i2_ref[...] = inverse
        y = normed * vec_ref[6:7] + vec_ref[7:8]
        row = lax.broadcasted_iota(jnp.int32, (SEG_LEN, 1), 0)
        out_ref[...] = jnp.where(row < live, y[0:SEG_LEN], 0.0)
        next_ref[...] = jnp.where(live > 0, y[SEG_LEN + PADM:ROWS], mem_ref[...])


def ffn_bwd_kernel(
    live_ref, cot_ref, dmem_ref, n1_ref, i1_ref, n2_ref, i2_ref, slope_ref, wo_ref, wu_ref, wd_ref, vec_ref,
    dfb_ref, dzb_ref, dob_ref, dr1_ref, da_ref, sums_ref,
    acc,
):
    step = pl.program_id(0)
    live = live_ref[0]

    @pl.when(step == 0)
    def _():
        row = lax.broadcasted_iota(jnp.int32, (SEG_LEN, 1), 0)
        token = jnp.where(row < live, cot_ref[...].astype(f32), 0.0)
        write = jnp.where(live > 0, dmem_ref[...], 0.0)
        dy = jnp.concatenate([token, jnp.zeros((PADM, D), f32), write], axis=0)
        normed = n2_ref[...]
        sums_ref[...] = jnp.zeros_like(sums_ref)
        sums_ref[6:7] = jnp.sum(dy * normed, axis=0, keepdims=True)
        sums_ref[7:8] = jnp.sum(dy, axis=0, keepdims=True)
        back = norm_back(dy, normed, i2_ref[...], vec_ref[6:7])
        low = back.astype(bf16)
        dfb_ref[...] = low
        sums_ref[5:6] = jnp.sum(low.astype(f32), axis=0, keepdims=True)
        acc[...] = back

    dz = (dot_nt(dfb_ref[...], wd_ref[...]) * slope_ref[...]).astype(bf16)
    dzb_ref[...] = dz
    sums_ref[pl.ds(8 + step, 1), :] = jnp.sum(dz.astype(f32), axis=0, keepdims=True)
    acc[...] += dot_nn(dz, wu_ref[...])

    @pl.when(step == CHUNKS - 1)
    def _():
        dh = acc[...]
        normed = n1_ref[...]
        sums_ref[3:4] = jnp.sum(dh * normed, axis=0, keepdims=True)
        sums_ref[4:5] = jnp.sum(dh, axis=0, keepdims=True)
        back = norm_back(dh, normed, i1_ref[...], vec_ref[3:4])
        dr1_ref[...] = back
        low = back.astype(bf16)
        dob_ref[...] = low
        sums_ref[2:3] = jnp.sum(low.astype(f32), axis=0, keepdims=True)
        da_ref[...] = dot_nt(low, wo_ref[...]).astype(bf16)


def attn_bwd_kernel(
    first, live_ref, q_ref, k_ref, v_ref, da_ref, lse_ref, dr1_ref, wq_ref, wk_ref, wv_ref,
    dq_ref, dk_ref, dv_ref, sums_ref, du_ref,
):
    live = live_ref[0]
    step = first + pl.program_id(0)

    @pl.when(step == first)
    def _():
        du_ref[...] = dr1_ref[...]

    valid = valid_positions((ROWS, 1), 0, live)
    for pair in range(COLS // 128):
        cols = slice(128 * pair, 128 * pair + 128)
        qp, kp, vp, dap = q_ref[:, cols], k_ref[:, cols], v_ref[:, cols], da_ref[:, cols]
        dq = dk = dv = None
        for half in range(2):
            head = step * (COLS // HEAD) + 2 * pair + half
            kh, vh, qh, dah = (mask_half(t, half) for t in (kp, vp, qp, dap))
            s = dot_nt(kh, qp)
            s = jnp.where(valid, s, neg_large)
            p = jnp.exp2(s * SCORE2 - lse_ref[pl.ds(head, 1), 0:ROWS])
            dp = dot_nt(vh, dap)
            inner = jnp.sum(p * dp, axis=0, keepdims=True)
            ds = (p * (dp - inner)).astype(bf16)
            parts = (dot_tn(ds, kh), dot_nn(ds, qh), dot_nn(p.astype(bf16), dah))
            if dq is None:
                dq, dk, dv = parts
            else:
                dq, dk, dv = dq + parts[0], dk + parts[1], dv + parts[2]
        dq_ref[:, cols] = (dq * ROOT).astype(bf16)
        dk_ref[:, cols] = (dk * ROOT).astype(bf16)
        dv_ref[:, cols] = dv.astype(bf16)
    dq, dk, dv = dq_ref[...], dk_ref[...], dv_ref[...]
    sums_ref[0:1] = jnp.sum(dq.astype(f32), axis=0, keepdims=True)
    sums_ref[1:2] = jnp.sum(dv.astype(f32), axis=0, keepdims=True)
    du_ref[...] += dot_nt(dq, wq_ref[...]) + dot_nt(dk, wk_ref[...]) + dot_nt(dv, wv_ref[...])


def grad_kernel(plan, count, *refs):
    out_ref = refs[count]
    step = pl.program_id(0)
    for index, pairs in enumerate(plan):
        @pl.when(step == index)
        def _(pairs=pairs):
            blocks = len(pairs[0][1])
            width = D // blocks
            for block in range(blocks):
                total = None
                for left, rights in pairs:
                    part = dot_tn(refs[left][...], refs[rights[block]][...])
                    total = part if total is None else total + part
                out_ref[:, width * block:width * block + width] = total.astype(bf16)


def spec(shape, index):
    return pl.BlockSpec(shape, index)


def whole(shape):
    return pl.BlockSpec(shape, lambda j: (0,) * len(shape))


SCALAR = pl.BlockSpec(memory_space=pltpu.SMEM)


def shape_of(shape, dtype):
    return jax.ShapeDtypeStruct(shape, dtype)


def params():
    return pltpu.CompilerParams(dimension_semantics=("arbitrary",), vmem_limit_bytes=VMEM_BYTES)


def cost(flops, moved):
    return pl.CostEstimate(flops=int(flops), bytes_accessed=int(moved), transcendentals=0)


def attn_fwd(segment, live, tokens, mem, weights, vectors):
    block = spec((ROWS, COLS), lambda j: (0, j))
    return pl.pallas_call(
        attn_fwd_kernel,
        grid=(STEPS,),
        in_specs=[
            SCALAR, spec((SEG_LEN, D), lambda j: (segment, 0)), whole((PADM, D)),
            spec((D, COLS), lambda j: (0, j)), spec((D, COLS), lambda j: (1, j)), spec((D, COLS), lambda j: (2, j)),
            spec((12, COLS), lambda j: (0, j)),
        ],
        out_specs=[whole((ROWS, D)), block, block, block, whole((16, ROWS_LANES)), block],
        out_shape=[shape_of((ROWS, D), bf16)] * 4 + [shape_of((16, ROWS_LANES), f32), shape_of((ROWS, D), bf16)],
        scratch_shapes=[pltpu.VMEM((ROWS_LANES, 128), f32)],
        compiler_params=params(),
        name="attn_fwd",
        cost_estimate=cost(5e9, 8e6),
    )(live, tokens, mem, weights, weights, weights, vectors)


def ffn_fwd(segment, live, tokens, mem, attended, weights, vectors):
    full = whole((ROWS, D))
    chunk = spec((ROWS, D), lambda j: (0, j))
    col = whole((ROWS, 1))
    return pl.pallas_call(
        ffn_fwd_kernel,
        grid=(CHUNKS,),
        in_specs=[
            SCALAR, spec((SEG_LEN, D), lambda j: (segment, 0)), whole((PADM, D)), full,
            spec((D, D), lambda j: (3, 0)), spec((D, D), lambda j: (4 + j, 0)), spec((D, D), lambda j: (8 + j, 0)),
            whole((12, D)),
        ],
        out_specs=[full, col, full, chunk, chunk, full, col, whole((SEG_LEN, D)), whole((PADM, D))],
        out_shape=[
            shape_of((ROWS, D), f32), shape_of((ROWS, 1), f32), shape_of((ROWS, D), bf16), shape_of((ROWS, FF), bf16),
            shape_of((ROWS, FF), f32), shape_of((ROWS, D), f32), shape_of((ROWS, 1), f32),
            shape_of((SEG_LEN, D), f32), shape_of((PADM, D), f32),
        ],
        scratch_shapes=[pltpu.VMEM((ROWS, D), f32)] * 2,
        compiler_params=params(),
        name="ffn_fwd",
        cost_estimate=cost(6e9, 25e6),
    )(live, tokens, mem, attended, weights, weights, weights, vectors)


def ffn_bwd(segment, live, cotangent, dmem, saved, weights, vectors):
    n1, i1, h1b, g, slope, n2, i2 = saved
    full = whole((ROWS, D))
    chunk = spec((ROWS, D), lambda j: (0, j))
    col = whole((ROWS, 1))
    return pl.pallas_call(
        ffn_bwd_kernel,
        grid=(CHUNKS,),
        in_specs=[
            SCALAR, spec((SEG_LEN, D), lambda j: (segment, 0)), whole((PADM, D)), full, col, full, col, chunk,
            spec((D, D), lambda j: (3, 0)), spec((D, D), lambda j: (4 + j, 0)), spec((D, D), lambda j: (8 + j, 0)),
            whole((12, D)),
        ],
        out_specs=[full, chunk, full, full, full, whole((12, D))],
        out_shape=[
            shape_of((ROWS, D), bf16), shape_of((ROWS, FF), bf16), shape_of((ROWS, D), bf16),
            shape_of((ROWS, D), f32), shape_of((ROWS, D), bf16), shape_of((12, D), f32),
        ],
        scratch_shapes=[pltpu.VMEM((ROWS, D), f32)],
        compiler_params=params(),
        name="ffn_bwd",
        cost_estimate=cost(6e9, 25e6),
    )(live, cotangent, dmem, n1, i1, n2, i2, slope, weights, weights, weights, vectors)


def attn_bwd(first, steps, live, q, k, v, da, lse, du, weights):
    block = spec((ROWS, COLS), lambda j: (0, first + j))
    own = spec((ROWS, COLS), lambda j: (0, j))
    return pl.pallas_call(
        functools.partial(attn_bwd_kernel, first),
        grid=(steps,),
        in_specs=[
            SCALAR, block, block, block, block, whole((16, ROWS_LANES)), whole((ROWS, D)),
            spec((D, COLS), lambda j: (0, first + j)), spec((D, COLS), lambda j: (1, first + j)),
            spec((D, COLS), lambda j: (2, first + j)),
        ],
        out_specs=[own, own, own, spec((8, COLS), lambda j: (0, j)), whole((ROWS, D))],
        out_shape=[shape_of((ROWS, steps * COLS), bf16)] * 3 + [
            shape_of((8, steps * COLS), f32), shape_of((ROWS, D), f32)],
        compiler_params=params(),
        name="attn_bwd",
        cost_estimate=cost(4e9, 5e6),
    )(live, q, k, v, da, lse, du, weights, weights, weights)


def grad_piece(products, name):
    arrays, specs, plan = [], [], []

    def add(array, chunk, width):
        for index, (have, *at) in enumerate(arrays):
            if have is array and at == [chunk, width]:
                return index
        arrays.append((array, chunk, width))
        specs.append(spec((ROWS, width), lambda j: (0, chunk)))
        return len(arrays) - 1

    def add_right(right):
        return [add(*part, COLS) for part in right] if isinstance(right, list) else [add(right, 0, D)]

    for lefts, chunk, rights in products:
        plan.append([(add(left, chunk, D), add_right(right)) for left, right in zip(lefts, rights)])
    return pl.pallas_call(
        functools.partial(grad_kernel, plan, len(arrays)),
        grid=(len(plan),),
        in_specs=specs,
        out_specs=spec((D, D), lambda j: (j, 0)),
        out_shape=shape_of((len(plan) * D, D), bf16),
        compiler_params=params(),
        name=name,
        cost_estimate=cost(4e9, 15e6),
    )(*[item[0] for item in arrays])


def rank_bits():
    place, line = lax.axis_index("dp"), lax.axis_index("fsdp")
    return {"y": place // 2, "x": place % 2, "z1": line // 4, "z0": (line // 2) % 2, "c": line % 2}


STRIDE = {"y": 16, "x": 8, "z1": 4, "z0": 2, "c": 1}


def swap(value, dims):
    mask = sum(STRIDE[dim] for dim in dims)
    return lax.ppermute(value, ("dp", "fsdp"), [(d, d ^ mask) for d in range(32)])


def add_low(left, right):
    return (left.astype(f32) + right.astype(f32)).astype(bf16)


class Reduction:
    def __init__(self, current, order, names=("z1", "z0", "c", "y", "x")):
        self.names, self.order, self.current = list(names), order, current
        if order:
            axis = self.names.index(order[0])
            bit = rank_bits()[order[0]]
            self.mine = lax.dynamic_index_in_dim(current, bit, axis, keepdims=False)
            self.other = lax.dynamic_index_in_dim(current, 1 - bit, axis, keepdims=False)

    @classmethod
    def of(cls, piece, order):
        return cls(piece.reshape((2,) * 5 + (-1, piece.shape[-1])), ("c",) + order)

    def add(self, got):
        names = [name for name in self.names if name != self.order[0]]
        return Reduction(add_low(self.mine, got), self.order[1:], names)

    def halves(self, right_order=None):
        width = self.current.shape[-1] // 2
        return (
            Reduction(self.current[..., :width], self.order, self.names),
            Reduction(self.current[..., width:], right_order or self.order, self.names),
        )


def joined(left, right):
    return Reduction(jnp.concatenate([left.current, right.current], axis=-1), left.order, left.names)


def beside(run, values, *reductions):
    flat, tree = jax.tree.flatten((values, [(r.mine, r.other) for r in reductions]))
    values, pairs = jax.tree.unflatten(tree, lax.optimization_barrier(tuple(flat)))
    gots = []
    for reduction, (mine, other) in zip(reductions, pairs):
        reduction.mine = mine
        gots.append(swap(other, (reduction.order[0],)))
    flat, tree = jax.tree.flatten((run(values), gots))
    result, gots = jax.tree.unflatten(tree, lax.optimization_barrier(tuple(flat)))
    return (result,) + tuple(r.add(got) for r, got in zip(reductions, gots))


def column_blocks(parts, index):
    return [(part[index], j) for part in parts for j in range(part[index].shape[1] // COLS)]


def spread(own):
    bits = rank_bits()
    place = lax.axis_index("dp")
    arrived = []
    for mask, dims in enumerate(((), ("x",), ("y",), ("x", "y"))):
        block = lax.dynamic_index_in_dim(own, place ^ mask, 0, keepdims=False)
        arrived.append(swap(block, dims) if dims else block)
    quarters = jnp.stack(arrived).reshape((2, 2) + arrived[0].shape)
    quarters = jnp.where(bits["y"] == 1, quarters[::-1], quarters)
    quarters = jnp.where(bits["x"] == 1, quarters[:, ::-1], quarters)
    return quarters.reshape(-1, D).astype(f32)


def adam_update(parameter, gradient, moment_one, moment_two, decay_factor):
    new_one = beta_one * moment_one + (1.0 - beta_one) * gradient
    new_two = beta_two * moment_two + (1.0 - beta_two) * gradient * gradient
    corrected_one = new_one / (1.0 - beta_one**adam_step)
    corrected_two = new_two / (1.0 - beta_two**adam_step)
    update = corrected_one / (jnp.sqrt(corrected_two) + adam_eps) + decay_factor * parameter
    return (update, new_one, new_two)


def local_grads(tokens, memory_init, chain_tokens, cotangent, weights, vectors):
    mem = jnp.pad(memory_init, ((0, PADM - MEM), (0, 0)))
    lives = [jnp.clip(chain_tokens - s * SEG_LEN, 0, SEG_LEN) for s in range(SEGS)]
    kept = []
    outputs = []
    for s in range(SEGS):
        x, q, k, v, lse, a = attn_fwd(s, lives[s], tokens, mem, weights, vectors)
        *saved, out, mem = ffn_fwd(s, lives[s], tokens, mem, a, weights, vectors)
        kept.append((x, q, k, v, lse, a, saved))
        outputs.append(out)
    dmem = jnp.zeros((PADM, D), f32)
    back = [None] * SEGS
    token_grads = [None] * SEGS
    pick = lambda items, i: [item[i] for item in items]
    x, a = pick(kept, 0), pick(kept, 5)
    h, g = ([k_[6][i] for k_ in kept] for i in (2, 3))
    custom = (lax.axis_size("dp"), lax.axis_size("fsdp")) == (4, 8)
    custom = (lax.axis_size("dp"), lax.axis_size("fsdp")) == (4, 8)
    for s in reversed(range(SEGS)):
        _, q, k, v, lse, _, saved = kept[s]
        dfb, dzb, dob, du, da, sums = ffn_bwd(s, lives[s], cotangent, dmem, saved, weights, vectors)
        back[s] = (dfb, dzb, dob, sums)
        parts = []

        def attend(state, steps=1, s=s, parts=parts):
            *part, out = attn_bwd(len(parts), steps, lives[s], *kept[s][1:4], *state, weights)
            parts.append(part)
            return (state[0], state[1], out)

        state = (da, lse, du)
        if s > 0:
            state = attend(state, STEPS)
            back[s] += (parts,)
        else:
            df, dz, do = (pick(back, i) for i in range(3))
            run_down = lambda df: grad_piece([(g, 1, df), (g, 2, df), (g, 3, df)], "grad_down")
            run_mixed = lambda dz: grad_piece([(dz, 2, h), (dz, 3, h), (g, 0, df)], "grad_mixed")
            run_up = lambda do: grad_piece([(a, 0, do), (dz, 0, h), (dz, 1, h)], "grad_up")
            back[0] += (parts,)
            run_qkv = lambda x: grad_piece(
                [(x, 0, [column_blocks(item[4], i) for item in back]) for i in range(3)], "grad_qkv")
            down = run_down(df)
            if not custom:
                mixed, up = run_mixed(dz), run_up(do)
                for _ in range(STEPS):
                    state = attend(state)
            else:
                r_down = Reduction.of(down, ("x", "y", "z0", "z1"))
                mixed, r_down = beside(run_mixed, dz, r_down)
                r_mixed = Reduction.of(mixed, ("z0", "y", "x", "z1"))
                down0, down1 = r_down.halves()
                up, down0, r_mixed = beside(run_up, do, down0, r_mixed)
                r_up = Reduction.of(up, ("x", "y", "z0", "z1"))
                mixed0, mixed1 = r_mixed.halves()
                state, down1, mixed0, r_up = beside(attend, state, down1, mixed0, r_up)
                r_down = joined(down0, down1)
                up0, up1 = r_up.halves()
                state, r_down, mixed1, up0 = beside(attend, state, r_down, mixed1, up0)
                r_mixed = joined(mixed0, mixed1)
                state, r_down, r_mixed, up1 = beside(attend, state, r_down, r_mixed, up1)
                r_up = joined(up0, up1)
        du = state[2]
        token_grads[s] = du[:SEG_LEN]
        dmem = du[SEG_LEN:SEG_LEN + PADM] + du[SEG_LEN + PADM:] + jnp.where(lives[s] > 0, 0.0, dmem)
    sums = sum(pick(back, 3))
    sums_qv = sum(jnp.concatenate([part[3] for part in item[4]], axis=1) for item in back)
    small = jnp.concatenate([sums_qv[0:2], sums[2:], dmem[:MEM]], axis=0)
    if custom:
        triple, r_down, r_mixed, r_up = beside(run_qkv, x, r_down, r_mixed, r_up)
        r_qkv = Reduction.of(triple, ("x", "y", "z0", "z1"))
        plus = lambda dim: (lambda value: value + swap(value, (dim,)))
        small, r_qkv, r_mixed, r_up = beside(plus("c"), small, r_qkv, r_mixed, r_up)
        qkv0, qkv1 = r_qkv.halves(("y", "x", "z0", "z1"))
        small, qkv0, qkv1, r_up = beside(plus("z0"), small, qkv0, qkv1, r_up)
        small, qkv0, qkv1 = beside(plus("z1"), small, qkv0, qkv1)
        small, r_qkv = beside(plus("x"), small, joined(qkv0, qkv1))
        small, r_qkv = beside(plus("y"), small, r_qkv)
        weight_sum = spread(jnp.stack([r.current for r in (r_qkv, r_up, r_mixed, r_down)]))
    else:
        total = jnp.concatenate([run_qkv(x), up, mixed, down], axis=0)
        weight_sum = lax.psum_scatter(total, ("dp", "fsdp"), scatter_dimension=0, tiled=True).astype(f32)
        small = lax.psum(small, ("dp", "fsdp"))
    return (jnp.concatenate(outputs, 0), jnp.concatenate(token_grads, 0), weight_sum, small)


def shards(
    tokens, memory_init, chain_tokens, cotangent, weights, weight_first, weight_second,
    vectors, vector_first, vector_second,
):
    axes = ("dp", "fsdp")
    total_chains = tokens.shape[0] * lax.axis_size(axes)
    grad_scale = float(total_chains * SEGS * SEG_LEN) ** (-0.5)
    gathered = lax.all_gather(weights.astype(bf16), axes, axis=0, tiled=True)
    output, token_grad, weight_sum, small = local_grads(
        tokens[0], memory_init, chain_tokens, cotangent[0], gathered, vectors)
    vector_sum, memory_sum = small[:-MEM], small[-MEM:]
    weight_grad = weight_sum * grad_scale
    vector_grad = vector_sum * grad_scale
    memory_grad = memory_sum * grad_scale
    weight_step, new_weight_first, new_weight_second = adam_update(
        weights, weight_grad, weight_first, weight_second, decay_rate)
    vector_step, new_vector_first, new_vector_second = adam_update(
        vectors, vector_grad, vector_first, vector_second, 0.0)
    return (
        output[None], token_grad[None], memory_grad, weight_grad, weight_step, new_weight_first, new_weight_second,
        vector_grad, vector_step, new_vector_first, new_vector_second,
    )


def solution(mesh):
    both = ("dp", "fsdp")
    chain = P(both, None, None)
    rows = P(both, None)
    return jax.shard_map(
        shards,
        mesh=mesh,
        in_specs=(chain, P(), P(both), chain, rows, rows, rows, P(), P(), P()),
        out_specs=(chain, chain, P(), rows, rows, rows, rows, P(), P(), P(), P()),
        check_vma=False,
    )
```

```python
import functools

import jax
import jax.numpy as jnp
from jax import lax
from jax.experimental import pallas as pl
from jax.experimental.layout import Layout, with_layout_constraint
from jax.experimental.pallas import tpu as pltpu
from jax.sharding import PartitionSpec as P

D = 768
HEADS = 12
HEAD = 64
FF = 3072
MEM = 10
SEG_LEN = 512
SEGS = 2
PADM = 16
ROWS = SEG_LEN + 2 * PADM
ROWS_LANES = -(-ROWS // 128) * 128
COLS = 256
STEPS = D // COLS
CHUNKS = FF // D

eps_norm = 1e-12
beta_one = 0.9
beta_two = 0.95
decay_rate = 0.1
adam_eps = 1e-08
adam_step = 10
neg_large = -1e30
LOG2E = 1.4426950408889634
SCORE2 = HEAD ** (-0.5) * LOG2E
ROOT = HEAD ** (-0.5)
f32 = jnp.float32
bf16 = jnp.bfloat16
VMEM_BYTES = 56 * 1024 * 1024


def dot_nn(left, right):
    return lax.dot_general(left, right, (((1,), (0,)), ((), ())), preferred_element_type=f32)


def dot_nt(left, right):
    return lax.dot_general(left, right, (((1,), (1,)), ((), ())), preferred_element_type=f32)


def dot_tn(left, right):
    return lax.dot_general(left, right, (((0,), (0,)), ((), ())), preferred_element_type=f32)


def valid_positions(shape, axis, live):
    at = lax.broadcasted_iota(jnp.int32, shape, axis)
    read = (at >= SEG_LEN) & (at < SEG_LEN + MEM)
    write = (at >= SEG_LEN + PADM) & (at < SEG_LEN + PADM + MEM)
    return (at < live) | read | write


def mask_half(values, half):
    lane = lax.broadcasted_iota(jnp.int32, values.shape, 1)
    keep = (lane < HEAD) if half == 0 else (lane >= HEAD)
    return jnp.where(keep, values, jnp.zeros_like(values))


def norm_rows(values):
    centred = values - jnp.mean(values, axis=-1, keepdims=True)
    inverse = lax.rsqrt(jnp.mean(centred * centred, axis=-1, keepdims=True) + eps_norm)
    return centred * inverse, inverse


def norm_back(gradient, normed, inverse, gain_row):
    scaled = gradient * gain_row
    centred = scaled - jnp.mean(scaled, axis=-1, keepdims=True)
    return inverse * (centred - normed * jnp.mean(scaled * normed, axis=-1, keepdims=True))


def gelu_parts(z):
    phi = 0.5 + 0.5 * lax.erf(z * 0.7071067811865476)
    return z * phi, phi + z * jnp.exp2(z * z * (-0.5 * LOG2E)) * 0.3989422804014327


def attn_fwd_kernel(
    live_ref, tok_ref, mem_ref, wq_ref, wk_ref, wv_ref, vec_ref,
    x_ref, q_ref, k_ref, v_ref, lse_ref, a_ref, lse_acc,
):
    step = pl.program_id(0)
    live = live_ref[0]

    @pl.when(step == 0)
    def _():
        x_ref[0:SEG_LEN] = tok_ref[...]
        low = mem_ref[...].astype(bf16)
        x_ref[SEG_LEN:SEG_LEN + PADM] = low
        x_ref[SEG_LEN + PADM:ROWS] = low
        lse_acc[...] = jnp.zeros_like(lse_acc)

    x = x_ref[...]
    q = (dot_nn(x, wq_ref[...]) + vec_ref[0:1]).astype(bf16)
    k = dot_nn(x, wk_ref[...]).astype(bf16)
    v = (dot_nn(x, wv_ref[...]) + vec_ref[1:2]).astype(bf16)
    q_ref[...] = q
    k_ref[...] = k
    v_ref[...] = v
    valid = valid_positions((1, ROWS), 1, live)
    lane = lax.broadcasted_iota(jnp.int32, (1, 128), 1)
    lse_all = lse_acc[0:ROWS]
    for pair in range(COLS // 128):
        cols = slice(128 * pair, 128 * pair + 128)
        qp, kp, vp = q[:, cols], k[:, cols], v[:, cols]
        total = None
        for half in range(2):
            s = dot_nt(qp, mask_half(kp, half))
            s = jnp.where(valid, s, neg_large)
            top = jnp.max(s, axis=1, keepdims=True)
            e = jnp.exp2((s - top) * SCORE2)
            amount = jnp.sum(e, axis=1, keepdims=True)
            p = (e * (1.0 / amount)).astype(bf16)
            lse = top * SCORE2 + jnp.log(amount) * LOG2E
            head = step * (COLS // HEAD) + 2 * pair + half
            lse_all = jnp.where(lane == head, lse, lse_all)
            part = dot_nn(p, mask_half(vp, half))
            total = part if total is None else total + part
        a_ref[:, cols] = total.astype(bf16)
    lse_acc[0:ROWS] = lse_all

    @pl.when(step == STEPS - 1)
    def _():
        lse_ref[...] = lse_acc[...].T[0:16]


def ffn_fwd_kernel(
    live_ref, tok_ref, mem_ref, a_ref, wo_ref, wu_ref, wd_ref, vec_ref, *refs,
):
    n1_ref, i1_ref, h1b_ref, g_ref, slope_ref, n2_ref, i2_ref, out_ref, next_ref, h1, acc = refs[-11:]
    step = pl.program_id(0)
    live = live_ref[0]

    @pl.when(step == 0)
    def _():
        branch = dot_nn(a_ref[...], wo_ref[...]) + vec_ref[2:3]
        mem = mem_ref[...]
        u = jnp.concatenate([tok_ref[...].astype(f32), mem, mem], axis=0)
        normed, inverse = norm_rows(u + branch)
        n1_ref[...] = normed
        i1_ref[...] = inverse
        full = normed * vec_ref[3:4] + vec_ref[4:5]
        h1[...] = full
        h1b_ref[...] = full.astype(bf16)
        acc[...] = full + vec_ref[5:6]

    bias = vec_ref[pl.ds(8 + step, 1), :]
    blocks = [slice(272 * i, 272 * i + 272) for i in range(2)]
    ahead = dot_nt(h1b_ref[blocks[0]], wu_ref[...]) + bias
    for index, rows in enumerate(blocks):
        z = ahead
        if index + 1 < len(blocks):
            ahead = dot_nt(h1b_ref[blocks[index + 1]], wu_ref[...]) + bias
        g, slope = gelu_parts(z)
        g = g.astype(bf16)
        g_ref[rows] = g
        slope_ref[rows] = slope
        acc[rows] += dot_nn(g, wd_ref[...])

    @pl.when(step == CHUNKS - 1)
    def _():
        normed, inverse = norm_rows(acc[...])
        n2_ref[...] = normed
        i2_ref[...] = inverse
        y = normed * vec_ref[6:7] + vec_ref[7:8]
        row = lax.broadcasted_iota(jnp.int32, (SEG_LEN, 1), 0)
        out_ref[...] = jnp.where(row < live, y[0:SEG_LEN], 0.0)
        next_ref[...] = jnp.where(live > 0, y[SEG_LEN + PADM:ROWS], mem_ref[...])


def ffn_bwd_kernel(
    live_ref, cot_ref, dmem_ref, n1_ref, i1_ref, n2_ref, i2_ref, slope_ref, wo_ref, wu_ref, wd_ref, vec_ref,
    dfb_ref, dzb_ref, dob_ref, dr1_ref, da_ref, sums_ref,
    acc,
):
    step = pl.program_id(0)
    live = live_ref[0]

    @pl.when(step == 0)
    def _():
        row = lax.broadcasted_iota(jnp.int32, (SEG_LEN, 1), 0)
        token = jnp.where(row < live, cot_ref[...].astype(f32), 0.0)
        write = jnp.where(live > 0, dmem_ref[...], 0.0)
        dy = jnp.concatenate([token, jnp.zeros((PADM, D), f32), write], axis=0)
        normed = n2_ref[...]
        sums_ref[...] = jnp.zeros_like(sums_ref)
        sums_ref[6:7] = jnp.sum(dy * normed, axis=0, keepdims=True)
        sums_ref[7:8] = jnp.sum(dy, axis=0, keepdims=True)
        back = norm_back(dy, normed, i2_ref[...], vec_ref[6:7])
        low = back.astype(bf16)
        dfb_ref[...] = low
        sums_ref[5:6] = jnp.sum(low.astype(f32), axis=0, keepdims=True)
        acc[...] = back

    dz = (dot_nt(dfb_ref[...], wd_ref[...]) * slope_ref[...]).astype(bf16)
    dzb_ref[...] = dz
    sums_ref[pl.ds(8 + step, 1), :] = jnp.sum(dz.astype(f32), axis=0, keepdims=True)
    acc[...] += dot_nn(dz, wu_ref[...])

    @pl.when(step == CHUNKS - 1)
    def _():
        dh = acc[...]
        normed = n1_ref[...]
        sums_ref[3:4] = jnp.sum(dh * normed, axis=0, keepdims=True)
        sums_ref[4:5] = jnp.sum(dh, axis=0, keepdims=True)
        back = norm_back(dh, normed, i1_ref[...], vec_ref[3:4])
        dr1_ref[...] = back
        low = back.astype(bf16)
        dob_ref[...] = low
        sums_ref[2:3] = jnp.sum(low.astype(f32), axis=0, keepdims=True)
        da_ref[...] = dot_nt(low, wo_ref[...]).astype(bf16)


def attn_bwd_kernel(
    first, live_ref, q_ref, k_ref, v_ref, da_ref, lse_ref, dr1_ref, wq_ref, wk_ref, wv_ref,
    dq_ref, dk_ref, dv_ref, sums_ref, du_ref,
):
    live = live_ref[0]
    step = first + pl.program_id(0)

    @pl.when(step == first)
    def _():
        du_ref[...] = dr1_ref[...]

    valid = valid_positions((ROWS, 1), 0, live)
    for pair in range(COLS // 128):
        cols = slice(128 * pair, 128 * pair + 128)
        qp, kp, vp, dap = q_ref[:, cols], k_ref[:, cols], v_ref[:, cols], da_ref[:, cols]
        dq = dk = dv = None
        for half in range(2):
            head = step * (COLS // HEAD) + 2 * pair + half
            kh, vh, qh, dah = (mask_half(t, half) for t in (kp, vp, qp, dap))
            s = dot_nt(kh, qp)
            s = jnp.where(valid, s, neg_large)
            p = jnp.exp2(s * SCORE2 - lse_ref[pl.ds(head, 1), 0:ROWS])
            dp = dot_nt(vh, dap)
            inner = jnp.sum(p * dp, axis=0, keepdims=True)
            ds = (p * (dp - inner)).astype(bf16)
            parts = (dot_tn(ds, kh), dot_nn(ds, qh), dot_nn(p.astype(bf16), dah))
            if dq is None:
                dq, dk, dv = parts
            else:
                dq, dk, dv = dq + parts[0], dk + parts[1], dv + parts[2]
        dq_ref[:, cols] = (dq * ROOT).astype(bf16)
        dk_ref[:, cols] = (dk * ROOT).astype(bf16)
        dv_ref[:, cols] = dv.astype(bf16)
    dq, dk, dv = dq_ref[...], dk_ref[...], dv_ref[...]
    sums_ref[0:1] = jnp.sum(dq.astype(f32), axis=0, keepdims=True)
    sums_ref[1:2] = jnp.sum(dv.astype(f32), axis=0, keepdims=True)
    du_ref[...] += dot_nt(dq, wq_ref[...]) + dot_nt(dk, wk_ref[...]) + dot_nt(dv, wv_ref[...])


def grad_kernel(plan, count, bits_ref, *refs):
    keep_ref, other_ref, made, sems = refs[count:]
    step = pl.program_id(0)
    core = bits_ref[BITS.index("c")]
    copies = []
    for index, pairs in enumerate(plan):
        ways = []
        for part in range(8):
            shard, third = divmod(8 * index + part, 3)
            source = made.at[index, pl.ds(96 * part, 96)]
            ways.append([
                pltpu.make_async_copy(source, target.at[shard // 2, pl.ds(96 * third, 96)], sems.at[index, part])
                for target in (keep_ref, other_ref)
            ])
        copies += ways

        @pl.when(step == index)
        def _(pairs=pairs, index=index, ways=ways):
            left = jnp.concatenate([refs[item][...] for item, _ in pairs], axis=0)
            blocks = len(pairs[0][1])
            width = D // blocks
            for block in range(blocks):
                right = jnp.concatenate([refs[items[block]][...] for _, items in pairs], axis=0)
                made[index, :, width * block:width * block + width] = dot_tn(left, right).astype(bf16)
            for part, (keep, other) in enumerate(ways):
                parity = (8 * index + part) // 3 % 2

                @pl.when(core == parity)
                def _(keep=keep):
                    keep.start()

                @pl.when(core != parity)
                def _(other=other):
                    other.start()

    @pl.when(step == len(plan) - 1)
    def _():
        for keep, _ in copies:
            keep.wait()


def spec(shape, index):
    return pl.BlockSpec(shape, index)


def whole(shape):
    return pl.BlockSpec(shape, lambda j: (0,) * len(shape))


SCALAR = pl.BlockSpec(memory_space=pltpu.SMEM)


def shape_of(shape, dtype):
    return jax.ShapeDtypeStruct(shape, dtype)


def params():
    return pltpu.CompilerParams(dimension_semantics=("arbitrary",), vmem_limit_bytes=VMEM_BYTES)


def cost(flops, moved):
    return pl.CostEstimate(flops=int(flops), bytes_accessed=int(moved), transcendentals=0)


def attn_fwd(segment, live, tokens, mem, weights, vectors):
    block = spec((ROWS, COLS), lambda j: (0, j))
    return pl.pallas_call(
        attn_fwd_kernel,
        grid=(STEPS,),
        in_specs=[
            SCALAR, spec((SEG_LEN, D), lambda j: (segment, 0)), whole((PADM, D)),
            spec((D, COLS), lambda j: (0, j)), spec((D, COLS), lambda j: (1, j)), spec((D, COLS), lambda j: (2, j)),
            spec((12, COLS), lambda j: (0, j)),
        ],
        out_specs=[whole((ROWS, D)), block, block, block, whole((16, ROWS_LANES)), block],
        out_shape=[shape_of((ROWS, D), bf16)] * 4 + [shape_of((16, ROWS_LANES), f32), shape_of((ROWS, D), bf16)],
        scratch_shapes=[pltpu.VMEM((ROWS_LANES, 128), f32)],
        compiler_params=params(),
        name="attn_fwd",
        cost_estimate=cost(5e9, 8e6),
    )(live, tokens, mem, weights, weights, weights, vectors)


def ffn_fwd(segment, live, tokens, mem, attended, weights, vectors, output):
    full = whole((ROWS, D))
    chunk = spec((ROWS, D), lambda j: (0, j))
    col = whole((ROWS, 1))
    return pl.pallas_call(
        ffn_fwd_kernel,
        grid=(CHUNKS,),
        in_specs=[
            SCALAR, spec((SEG_LEN, D), lambda j: (segment, 0)), whole((PADM, D)), full,
            spec((D, D), lambda j: (3, 0)), spec((D, D), lambda j: (4 + j, 0)), spec((D, D), lambda j: (8 + j, 0)),
            whole((12, D)),
        ] + [pl.BlockSpec(memory_space=pl.ANY)] * (output is not None),
        out_specs=[full, col, full, chunk, chunk, full, col, spec((SEG_LEN, D), lambda j: (segment, 0)), whole((PADM, D))],
        out_shape=[
            shape_of((ROWS, D), f32), shape_of((ROWS, 1), f32), shape_of((ROWS, D), bf16), shape_of((ROWS, FF), bf16),
            shape_of((ROWS, FF), f32), shape_of((ROWS, D), f32), shape_of((ROWS, 1), f32),
            shape_of((SEGS * SEG_LEN, D), f32), shape_of((PADM, D), f32),
        ],
        input_output_aliases={} if output is None else {8: 7},
        scratch_shapes=[pltpu.VMEM((ROWS, D), f32)] * 2,
        compiler_params=params(),
        name="ffn_fwd",
        cost_estimate=cost(6e9, 25e6),
    )(live, tokens, mem, attended, weights, weights, weights, vectors, *([] if output is None else [output]))


def ffn_bwd(segment, live, cotangent, dmem, saved, weights, vectors):
    n1, i1, h1b, g, slope, n2, i2 = saved
    full = whole((ROWS, D))
    chunk = spec((ROWS, D), lambda j: (0, j))
    col = whole((ROWS, 1))
    return pl.pallas_call(
        ffn_bwd_kernel,
        grid=(CHUNKS,),
        in_specs=[
            SCALAR, spec((SEG_LEN, D), lambda j: (segment, 0)), whole((PADM, D)), full, col, full, col, chunk,
            spec((D, D), lambda j: (3, 0)), spec((D, D), lambda j: (4 + j, 0)), spec((D, D), lambda j: (8 + j, 0)),
            whole((12, D)),
        ],
        out_specs=[full, chunk, full, full, full, whole((12, D))],
        out_shape=[
            shape_of((ROWS, D), bf16), shape_of((ROWS, FF), bf16), shape_of((ROWS, D), bf16),
            shape_of((ROWS, D), f32), shape_of((ROWS, D), bf16), shape_of((12, D), f32),
        ],
        scratch_shapes=[pltpu.VMEM((ROWS, D), f32)],
        compiler_params=params(),
        name="ffn_bwd",
        cost_estimate=cost(6e9, 25e6),
    )(live, cotangent, dmem, n1, i1, n2, i2, slope, weights, weights, weights, vectors)


def attn_bwd(first, steps, live, q, k, v, da, lse, du, weights):
    block = spec((ROWS, COLS), lambda j: (0, first + j))
    own = spec((ROWS, COLS), lambda j: (0, j))
    return pl.pallas_call(
        functools.partial(attn_bwd_kernel, first),
        grid=(steps,),
        in_specs=[
            SCALAR, block, block, block, block, whole((16, ROWS_LANES)), whole((ROWS, D)),
            spec((D, COLS), lambda j: (0, first + j)), spec((D, COLS), lambda j: (1, first + j)),
            spec((D, COLS), lambda j: (2, first + j)),
        ],
        out_specs=[own, own, own, spec((8, COLS), lambda j: (0, j)), whole((ROWS, D))],
        out_shape=[shape_of((ROWS, steps * COLS), bf16)] * 3 + [
            shape_of((8, steps * COLS), f32), shape_of((ROWS, D), f32)],
        compiler_params=params(),
        name="attn_bwd",
        cost_estimate=cost(4e9, 5e6),
    )(live, q, k, v, da, lse, du, weights, weights, weights)


def grad_piece(products, name):
    arrays, specs, plan = [], [], []

    def add(array, chunk, width):
        for index, (have, *at) in enumerate(arrays):
            if have is array and at == [chunk, width]:
                return index
        arrays.append((array, chunk, width))
        specs.append(spec((ROWS, width), lambda j: (0, chunk)))
        return len(arrays) - 1

    def add_right(right):
        return [add(*part, COLS) for part in right] if isinstance(right, list) else [add(right, 0, D)]

    for lefts, chunk, rights in products:
        plan.append([(add(left, chunk, D), add_right(right)) for left, right in zip(lefts, rights)])
    anywhere = pl.BlockSpec(memory_space=pl.ANY)
    return pl.pallas_call(
        functools.partial(grad_kernel, plan, len(arrays)),
        grid=(len(plan),),
        in_specs=[SCALAR] + specs,
        out_specs=[anywhere] * 2,
        out_shape=[shape_of((4, 288, D), bf16)] * 2,
        scratch_shapes=[pltpu.VMEM((3, D, D), bf16), pltpu.SemaphoreType.DMA((3, 8))],
        compiler_params=params(),
        name=name,
        cost_estimate=cost(4e9, 15e6),
    )(rank_bits(), *[item[0] for item in arrays])


BITS = ("y", "x", "z1", "z0", "c")


def rank_bits():
    place, line = lax.axis_index("dp"), lax.axis_index("fsdp")
    return jnp.stack([place // 2 % 2, place % 2, line // 4 % 2, line // 2 % 2, line % 2]).astype(jnp.int32)


STRIDE = {"y": 16, "x": 8, "z1": 4, "z0": 2, "c": 1}


def swap(value, dims):
    mask = sum(STRIDE[dim] for dim in dims)
    return lax.ppermute(value, ("dp", "fsdp"), [(d, d ^ mask) for d in range(32)])


def add_low(left, right):
    return (left.astype(f32) + right.astype(f32)).astype(bf16)


class Part:
    def __init__(self, keeps, gots, names, dim, split=False):
        self.keeps, self.gots, self.names, self.dim, self.split = keeps, gots, names, dim, split


def columns(items):
    cut = [array[..., block * size:(block + 1) * size] for array, block, size in items]
    return cut[0] if len(cut) == 1 else jnp.concatenate(cut, axis=-1)


def combine(*parts):
    made = []
    for part in parts:
        keep, got = columns(part.keeps), columns(part.gots)
        if part.dim is None:
            made.append(add_low(keep, got))
            continue
        axis = part.names.index(part.dim)
        bit = rank_bits()[BITS.index(part.dim)]
        stays, goes = (
            add_low(*(lax.dynamic_index_in_dim(item, at, axis, keepdims=False) for item in (keep, got)))
            for at in (bit, 1 - bit))
        made.append(stays)
        width = goes.shape[-1] // 2
        made += [goes[..., :width], goes[..., width:]] if part.split else [goes]
    return made


def row_major(array):
    return with_layout_constraint(array, Layout(major_to_minor=tuple(range(array.ndim))))


def exchange(run, values, *sends):
    flat, tree = jax.tree.flatten((values, [array for array, _ in sends]))
    values, arrays = jax.tree.unflatten(tree, lax.optimization_barrier(tuple(flat)))
    arrays = [row_major(array) for array in arrays]
    gots = [row_major(swap(array, (dim,))) for array, (_, dim) in zip(arrays, sends)]
    flat, tree = jax.tree.flatten((run(values), gots))
    result, gots = jax.tree.unflatten(tree, lax.optimization_barrier(tuple(flat)))
    return (result,) + tuple(gots)


def unsplit(pair, parity):
    keep, other = pair
    even, odd = jnp.where(parity == 0, keep, other), jnp.where(parity == 0, other, keep)
    return jnp.stack([even, odd], axis=1).reshape(-1, D)


def column_blocks(parts, index):
    return [(part[index], j) for part in parts for j in range(part[index].shape[1] // COLS)]


def spread(own):
    place = lax.axis_index("dp")
    arrived = []
    for mask, dims in enumerate(((), ("x",), ("y",), ("x", "y"))):
        block = lax.dynamic_index_in_dim(own, place ^ mask, 0, keepdims=False)
        arrived.append(swap(block, dims) if dims else block)
    quarters = jnp.stack(arrived).reshape((2, 2) + arrived[0].shape)
    quarters = jnp.where(place // 2 == 1, quarters[::-1], quarters)
    quarters = jnp.where(place % 2 == 1, quarters[:, ::-1], quarters)
    return quarters.reshape(-1, D).astype(f32)


def adam_update(parameter, gradient, moment_one, moment_two, decay_factor):
    new_one = beta_one * moment_one + (1.0 - beta_one) * gradient
    new_two = beta_two * moment_two + (1.0 - beta_two) * gradient * gradient
    corrected_one = new_one / (1.0 - beta_one**adam_step)
    corrected_two = new_two / (1.0 - beta_two**adam_step)
    update = corrected_one / (jnp.sqrt(corrected_two) + adam_eps) + decay_factor * parameter
    return (update, new_one, new_two)


def local_grads(tokens, memory_init, chain_tokens, cotangent, weights, vectors):
    mem = jnp.pad(memory_init, ((0, PADM - MEM), (0, 0)))
    lives = [jnp.clip(chain_tokens - s * SEG_LEN, 0, SEG_LEN) for s in range(SEGS)]
    kept = []
    out = None
    for s in range(SEGS):
        x, q, k, v, lse, a = attn_fwd(s, lives[s], tokens, mem, weights, vectors)
        *saved, out, mem = ffn_fwd(s, lives[s], tokens, mem, a, weights, vectors, out)
        kept.append((x, q, k, v, lse, a, saved))
    dmem = jnp.zeros((PADM, D), f32)
    back = [None] * SEGS
    token_grads = [None] * SEGS
    pick = lambda items, i: [item[i] for item in items]
    x, a = pick(kept, 0), pick(kept, 5)
    h, g = ([k_[6][i] for k_ in kept] for i in (2, 3))
    custom = (lax.axis_size("dp"), lax.axis_size("fsdp")) == (4, 8)
    custom = (lax.axis_size("dp"), lax.axis_size("fsdp")) == (4, 8)
    for s in reversed(range(SEGS)):
        _, q, k, v, lse, _, saved = kept[s]
        dfb, dzb, dob, du, da, sums = ffn_bwd(s, lives[s], cotangent, dmem, saved, weights, vectors)
        back[s] = (dfb, dzb, dob, sums)
        parts = []

        def attend(state, steps=1, s=s, parts=parts):
            *part, out = attn_bwd(len(parts), steps, lives[s], *kept[s][1:4], *state, weights)
            parts.append(part)
            return (state[0], state[1], out)

        state = (da, lse, du)
        if s > 0:
            state = attend(state, STEPS)
            back[s] += (parts,)
        else:
            df, dz, do = (pick(back, i) for i in range(3))
            run_down = lambda df: grad_piece([(g, 1, df), (g, 2, df), (g, 3, df)], "grad_down")
            run_mixed = lambda dz: grad_piece([(dz, 2, h), (dz, 3, h), (g, 0, df)], "grad_mixed")
            run_up = lambda do: grad_piece([(a, 0, do), (dz, 0, h), (dz, 1, h)], "grad_up")
            back[0] += (parts,)
            run_qkv = lambda x: grad_piece(
                [(x, 0, [column_blocks(item[4], i) for item in back]) for i in range(3)], "grad_qkv")
            down = run_down(df)
            if not custom:
                mixed, up = run_mixed(dz), run_up(do)
                for _ in range(STEPS):
                    state = attend(state)
            else:
                full = lambda *items: [(item, 0, item.shape[-1]) for item in items]
                view = lambda item: item.reshape((2,) * 4 + (72, D))
                plane = ["z1", "z0", "y", "x"]
                d_keep, d_send = map(view, down)
                mixed, d_got = exchange(run_mixed, dz, (d_send, "c"))
                d_keep, d_left, d_right = combine(Part(full(d_keep), full(d_got), plane, "x", True))
                m_keep, m_send = map(view, mixed)
                up, d_got, m_got = exchange(run_up, do, (d_left, "x"), (m_send, "c"))
                m_keep, m_left, m_right = combine(Part(full(m_keep), full(m_got), plane, "z0", True))
                u_keep, u_send = map(view, up)
                state, d_more, m_got, u_got = exchange(attend, state, (d_right, "x"), (m_left, "z0"), (u_send, "c"))
                d_keep, d_send, u_keep, u_left, u_right = combine(
                    Part(full(d_keep), full(d_got, d_more), ["z1", "z0", "y"], "y"),
                    Part(full(u_keep), full(u_got), plane, "x", True))
                state, d_got, m_more, u_got = exchange(attend, state, (d_send, "y"), (m_right, "z0"), (u_left, "x"))
                d_keep, d_send, m_keep, m_send = combine(
                    Part(full(d_keep), full(d_got), ["z1", "z0"], "z0"),
                    Part(full(m_keep), full(m_got, m_more), ["z1", "y", "x"], "y"))
                state, d_got, m_got, u_more = exchange(attend, state, (d_send, "z0"), (m_send, "y"), (u_right, "x"))
                d_keep, d_send, m_keep, m_send, u_keep, u_send = combine(
                    Part(full(d_keep), full(d_got), ["z1"], "z1"),
                    Part(full(m_keep), full(m_got), ["z1", "x"], "x"),
                    Part(full(u_keep), full(u_got, u_more), ["z1", "z0", "y"], "y"))
        du = state[2]
        token_grads[s] = du[:SEG_LEN]
        dmem = du[SEG_LEN:SEG_LEN + PADM] + du[SEG_LEN + PADM:] + jnp.where(lives[s] > 0, 0.0, dmem)
    sums = sum(pick(back, 3))
    sums_qv = sum(jnp.concatenate([part[3] for part in item[4]], axis=1) for item in back)
    small = jnp.concatenate([sums_qv[0:2], sums[2:], dmem[:MEM]], axis=0)
    if custom:
        triple, d_got, m_got, u_got = exchange(run_qkv, x, (d_send, "z1"), (m_send, "x"), (u_send, "y"))
        m_keep, m_send, u_keep, u_send = combine(
            Part(full(m_keep), full(m_got), ["z1"], "z1"), Part(full(u_keep), full(u_got), ["z1", "z0"], "z0"))
        plus = lambda dim: (lambda value: value + swap(value, (dim,)))
        t_keep, t_send = map(view, triple)
        small, t_got, m_got, u_got = exchange(plus("c"), small, (t_send, "c"), (m_send, "z1"), (u_send, "z0"))
        halves = lambda item: [[(item, i, D // 2)] for i in range(2)]
        (k0, k1), (g0, g1) = halves(t_keep), halves(t_got)
        k0, s0, k1, s1, u_keep, u_send = combine(
            Part(k0, g0, plane, "x"), Part(k1, g1, plane, "y"), Part(full(u_keep), full(u_got), ["z1"], "z1"))
        small, g0, g1, u_got = exchange(plus("z0"), small, (s0, "x"), (s1, "y"), (u_send, "z1"))
        k0, s0, k1, s1 = combine(
            Part(full(k0), full(g0), ["z1", "z0", "y"], "y"), Part(full(k1), full(g1), ["z1", "z0", "x"], "x"))
        small, g0, g1 = exchange(plus("z1"), small, (s0, "y"), (s1, "x"))
        t_keep, t_send = combine(Part(full(k0, k1), full(g0, g1), ["z1", "z0"], "z0"))
        small, t_got = exchange(plus("x"), small, (t_send, "z0"))
        t_keep, t_send = combine(Part(full(t_keep), full(t_got), ["z1"], "z1"))
        small, t_got = exchange(plus("y"), small, (t_send, "z1"))
        own = combine(*(Part(full(k), full(g), [], None) for k, g in (
            (t_keep, t_got), (u_keep, u_got), (m_keep, m_got), (d_keep, d_got))))
        weight_sum = spread(jnp.stack(own))
    else:
        parity = lax.axis_index("fsdp") % 2
        total = jnp.concatenate([unsplit(item, parity) for item in (run_qkv(x), up, mixed, down)], axis=0)
        weight_sum = lax.psum_scatter(total, ("dp", "fsdp"), scatter_dimension=0, tiled=True).astype(f32)
        small = lax.psum(small, ("dp", "fsdp"))
    return (out, jnp.concatenate(token_grads, 0), weight_sum, small)


def shards(
    tokens, memory_init, chain_tokens, cotangent, weights, weight_first, weight_second,
    vectors, vector_first, vector_second,
):
    axes = ("dp", "fsdp")
    total_chains = tokens.shape[0] * lax.axis_size(axes)
    grad_scale = float(total_chains * SEGS * SEG_LEN) ** (-0.5)
    gathered = lax.all_gather(weights.astype(bf16), axes, axis=0, tiled=True)
    output, token_grad, weight_sum, small = local_grads(
        tokens[0], memory_init, chain_tokens, cotangent[0], gathered, vectors)
    vector_sum, memory_sum = small[:-MEM], small[-MEM:]
    weight_grad = weight_sum * grad_scale
    vector_grad = vector_sum * grad_scale
    memory_grad = memory_sum * grad_scale
    weight_step, new_weight_first, new_weight_second = adam_update(
        weights, weight_grad, weight_first, weight_second, decay_rate)
    vector_step, new_vector_first, new_vector_second = adam_update(
        vectors, vector_grad, vector_first, vector_second, 0.0)
    return (
        output[None], token_grad[None], memory_grad, weight_grad, weight_step, new_weight_first, new_weight_second,
        vector_grad, vector_step, new_vector_first, new_vector_second,
    )


def solution(mesh):
    both = ("dp", "fsdp")
    chain = P(both, None, None)
    rows = P(both, None)
    return jax.shard_map(
        shards,
        mesh=mesh,
        in_specs=(chain, P(), P(both), chain, rows, rows, rows, P(), P(), P()),
        out_specs=(chain, chain, P(), rows, rows, rows, rows, P(), P(), P(), P()),
        check_vma=False,
    )
```

```python
import functools

import jax
import jax.numpy as jnp
from jax import lax
from jax.experimental import pallas as pl
from jax.experimental.layout import Layout, with_layout_constraint
from jax.experimental.pallas import tpu as pltpu
from jax.sharding import PartitionSpec as P

D = 768
HEADS = 12
HEAD = 64
FF = 3072
MEM = 10
SEG_LEN = 512
SEGS = 2
PADM = 16
ROWS = SEG_LEN + 2 * PADM
ROWS_LANES = -(-ROWS // 128) * 128
COLS = 256
STEPS = D // COLS
CHUNKS = FF // D

eps_norm = 1e-12
beta_one = 0.9
beta_two = 0.95
decay_rate = 0.1
adam_eps = 1e-08
adam_step = 10
neg_large = -1e30
LOG2E = 1.4426950408889634
SCORE2 = HEAD ** (-0.5) * LOG2E
ROOT = HEAD ** (-0.5)
f32 = jnp.float32
bf16 = jnp.bfloat16
VMEM_BYTES = 56 * 1024 * 1024


def dot_nn(left, right):
    return lax.dot_general(left, right, (((1,), (0,)), ((), ())), preferred_element_type=f32)


def dot_nt(left, right):
    return lax.dot_general(left, right, (((1,), (1,)), ((), ())), preferred_element_type=f32)


def dot_tn(left, right):
    return lax.dot_general(left, right, (((0,), (0,)), ((), ())), preferred_element_type=f32)


def valid_positions(shape, axis, live):
    at = lax.broadcasted_iota(jnp.int32, shape, axis)
    read = (at >= SEG_LEN) & (at < SEG_LEN + MEM)
    write = (at >= SEG_LEN + PADM) & (at < SEG_LEN + PADM + MEM)
    return (at < live) | read | write


def mask_half(values, half):
    lane = lax.broadcasted_iota(jnp.int32, values.shape, 1)
    keep = (lane < HEAD) if half == 0 else (lane >= HEAD)
    return jnp.where(keep, values, jnp.zeros_like(values))


def norm_rows(values):
    centred = values - jnp.mean(values, axis=-1, keepdims=True)
    inverse = lax.rsqrt(jnp.mean(centred * centred, axis=-1, keepdims=True) + eps_norm)
    return centred * inverse, inverse


def norm_back(gradient, normed, inverse, gain_row):
    scaled = gradient * gain_row
    centred = scaled - jnp.mean(scaled, axis=-1, keepdims=True)
    return inverse * (centred - normed * jnp.mean(scaled * normed, axis=-1, keepdims=True))


def gelu_parts(z):
    phi = 0.5 + 0.5 * lax.erf(z * 0.7071067811865476)
    return z * phi, phi + z * jnp.exp2(z * z * (-0.5 * LOG2E)) * 0.3989422804014327


def attn_fwd_kernel(
    live_ref, tok_ref, mem_ref, wq_ref, wk_ref, wv_ref, vec_ref,
    x_ref, q_ref, k_ref, v_ref, lse_ref, a_ref, lse_acc,
):
    step = pl.program_id(0)
    live = live_ref[0]

    @pl.when(step == 0)
    def _():
        x_ref[0:SEG_LEN] = tok_ref[...]
        low = mem_ref[...].astype(bf16)
        x_ref[SEG_LEN:SEG_LEN + PADM] = low
        x_ref[SEG_LEN + PADM:ROWS] = low
        lse_acc[...] = jnp.zeros_like(lse_acc)

    x = x_ref[...]
    q = (dot_nn(x, wq_ref[...]) + vec_ref[0:1]).astype(bf16)
    k = dot_nn(x, wk_ref[...]).astype(bf16)
    v = (dot_nn(x, wv_ref[...]) + vec_ref[1:2]).astype(bf16)
    q_ref[...] = q
    k_ref[...] = k
    v_ref[...] = v
    valid = valid_positions((1, ROWS), 1, live)
    lane = lax.broadcasted_iota(jnp.int32, (1, 128), 1)
    lse_all = lse_acc[0:ROWS]
    for pair in range(COLS // 128):
        cols = slice(128 * pair, 128 * pair + 128)
        qp, kp, vp = q[:, cols], k[:, cols], v[:, cols]
        total = None
        for half in range(2):
            s = dot_nt(qp, mask_half(kp, half))
            s = jnp.where(valid, s, neg_large)
            top = jnp.max(s, axis=1, keepdims=True)
            e = jnp.exp2((s - top) * SCORE2)
            amount = jnp.sum(e, axis=1, keepdims=True)
            p = (e * (1.0 / amount)).astype(bf16)
            lse = top * SCORE2 + jnp.log(amount) * LOG2E
            head = step * (COLS // HEAD) + 2 * pair + half
            lse_all = jnp.where(lane == head, lse, lse_all)
            part = dot_nn(p, mask_half(vp, half))
            total = part if total is None else total + part
        a_ref[:, cols] = total.astype(bf16)
    lse_acc[0:ROWS] = lse_all

    @pl.when(step == STEPS - 1)
    def _():
        lse_ref[...] = lse_acc[...].T[0:16]


def ffn_fwd_kernel(
    live_ref, tok_ref, mem_ref, a_ref, wo_ref, wu_ref, wd_ref, vec_ref, *refs,
):
    n1_ref, i1_ref, h1b_ref, g_ref, slope_ref, n2_ref, i2_ref, out_ref, next_ref, h1, acc = refs[-11:]
    step = pl.program_id(0)
    live = live_ref[0]

    @pl.when(step == 0)
    def _():
        branch = dot_nn(a_ref[...], wo_ref[...]) + vec_ref[2:3]
        mem = mem_ref[...]
        u = jnp.concatenate([tok_ref[...].astype(f32), mem, mem], axis=0)
        normed, inverse = norm_rows(u + branch)
        n1_ref[...] = normed.astype(bf16)
        i1_ref[...] = inverse
        full = normed * vec_ref[3:4] + vec_ref[4:5]
        h1[...] = full
        h1b_ref[...] = full.astype(bf16)
        acc[...] = full + vec_ref[5:6]

    bias = vec_ref[pl.ds(8 + step, 1), :]
    blocks = [slice(272 * i, 272 * i + 272) for i in range(2)]
    ahead = dot_nt(h1b_ref[blocks[0]], wu_ref[...]) + bias
    for index, rows in enumerate(blocks):
        z = ahead
        if index + 1 < len(blocks):
            ahead = dot_nt(h1b_ref[blocks[index + 1]], wu_ref[...]) + bias
        g, slope = gelu_parts(z)
        g = g.astype(bf16)
        g_ref[rows] = g
        slope_ref[rows] = slope.astype(bf16)
        acc[rows] += dot_nn(g, wd_ref[...])

    @pl.when(step == CHUNKS - 1)
    def _():
        normed, inverse = norm_rows(acc[...])
        n2_ref[...] = normed.astype(bf16)
        i2_ref[...] = inverse
        y = normed * vec_ref[6:7] + vec_ref[7:8]
        row = lax.broadcasted_iota(jnp.int32, (SEG_LEN, 1), 0)
        out_ref[...] = jnp.where(row < live, y[0:SEG_LEN], 0.0)
        next_ref[...] = jnp.where(live > 0, y[SEG_LEN + PADM:ROWS], mem_ref[...])


def ffn_bwd_kernel(
    live_ref, cot_ref, dmem_ref, n1_ref, i1_ref, n2_ref, i2_ref, slope_ref, wo_ref, wu_ref, wd_ref, vec_ref,
    dfb_ref, dzb_ref, dob_ref, dr1_ref, da_ref, sums_ref,
    acc,
):
    step = pl.program_id(0)
    live = live_ref[0]

    @pl.when(step == 0)
    def _():
        row = lax.broadcasted_iota(jnp.int32, (SEG_LEN, 1), 0)
        token = jnp.where(row < live, cot_ref[...].astype(f32), 0.0)
        write = jnp.where(live > 0, dmem_ref[...], 0.0)
        dy = jnp.concatenate([token, jnp.zeros((PADM, D), f32), write], axis=0)
        normed = n2_ref[...].astype(f32)
        sums_ref[...] = jnp.zeros_like(sums_ref)
        sums_ref[6:7] = jnp.sum(dy * normed, axis=0, keepdims=True)
        sums_ref[7:8] = jnp.sum(dy, axis=0, keepdims=True)
        back = norm_back(dy, normed, i2_ref[...], vec_ref[6:7])
        low = back.astype(bf16)
        dfb_ref[...] = low
        sums_ref[5:6] = jnp.sum(low.astype(f32), axis=0, keepdims=True)
        acc[...] = back

    blocks = [slice(ROWS // 2 * i, ROWS // 2 * (i + 1)) for i in range(2)]
    ahead = dot_nt(dfb_ref[blocks[0]], wd_ref[...])
    total = None
    for index, rows in enumerate(blocks):
        dg = ahead
        if index + 1 < len(blocks):
            ahead = dot_nt(dfb_ref[blocks[index + 1]], wd_ref[...])
        dz = (dg * slope_ref[rows].astype(f32)).astype(bf16)
        dzb_ref[rows] = dz
        part = jnp.sum(dz.astype(f32), axis=0, keepdims=True)
        total = part if total is None else total + part
        acc[rows] += dot_nn(dz, wu_ref[...])
    sums_ref[pl.ds(8 + step, 1), :] = total

    @pl.when(step == CHUNKS - 1)
    def _():
        dh = acc[...]
        normed = n1_ref[...].astype(f32)
        sums_ref[3:4] = jnp.sum(dh * normed, axis=0, keepdims=True)
        sums_ref[4:5] = jnp.sum(dh, axis=0, keepdims=True)
        back = norm_back(dh, normed, i1_ref[...], vec_ref[3:4])
        dr1_ref[...] = back
        low = back.astype(bf16)
        dob_ref[...] = low
        sums_ref[2:3] = jnp.sum(low.astype(f32), axis=0, keepdims=True)
        da_ref[...] = dot_nt(low, wo_ref[...]).astype(bf16)


def attn_bwd_kernel(
    first, live_ref, q_ref, k_ref, v_ref, da_ref, lse_ref, dr1_ref, wq_ref, wk_ref, wv_ref,
    dq_ref, dk_ref, dv_ref, sums_ref, du_ref,
):
    live = live_ref[0]
    step = first + pl.program_id(0)

    @pl.when(step == first)
    def _():
        du_ref[...] = dr1_ref[...]

    valid = valid_positions((ROWS, 1), 0, live)
    for pair in range(COLS // 128):
        cols = slice(128 * pair, 128 * pair + 128)
        qp, kp, vp, dap = q_ref[:, cols], k_ref[:, cols], v_ref[:, cols], da_ref[:, cols]
        dq = dk = dv = None
        for half in range(2):
            head = step * (COLS // HEAD) + 2 * pair + half
            kh, vh, qh, dah = (mask_half(t, half) for t in (kp, vp, qp, dap))
            s = dot_nt(kh, qp)
            s = jnp.where(valid, s, neg_large)
            p = jnp.exp2(s * SCORE2 - lse_ref[pl.ds(head, 1), 0:ROWS])
            dp = dot_nt(vh, dap)
            inner = jnp.sum(p * dp, axis=0, keepdims=True)
            ds = (p * (dp - inner)).astype(bf16)
            parts = (dot_tn(ds, kh), dot_nn(ds, qh), dot_nn(p.astype(bf16), dah))
            if dq is None:
                dq, dk, dv = parts
            else:
                dq, dk, dv = dq + parts[0], dk + parts[1], dv + parts[2]
        dq_ref[:, cols] = (dq * ROOT).astype(bf16)
        dk_ref[:, cols] = (dk * ROOT).astype(bf16)
        dv_ref[:, cols] = dv.astype(bf16)
    dq, dk, dv = dq_ref[...], dk_ref[...], dv_ref[...]
    sums_ref[0:1] = jnp.sum(dq.astype(f32), axis=0, keepdims=True)
    sums_ref[1:2] = jnp.sum(dv.astype(f32), axis=0, keepdims=True)
    du_ref[...] += dot_nt(dq, wq_ref[...]) + dot_nt(dk, wk_ref[...]) + dot_nt(dv, wv_ref[...])


def grad_kernel(plan, count, bits_ref, *refs):
    keep_ref, other_ref, made, sems = refs[count:]
    step = pl.program_id(0)
    core = bits_ref[BITS.index("c")]
    copies = []
    for index, pairs in enumerate(plan):
        ways = []
        for part in range(8):
            shard, third = divmod(8 * index + part, 3)
            source = made.at[index, pl.ds(96 * part, 96)]
            ways.append([
                pltpu.make_async_copy(source, target.at[shard // 2, pl.ds(96 * third, 96)], sems.at[index, part])
                for target in (keep_ref, other_ref)
            ])
        copies += ways

        @pl.when(step == index)
        def _(pairs=pairs, index=index, ways=ways):
            left = jnp.concatenate([refs[item][...] for item, _ in pairs], axis=0)
            blocks = len(pairs[0][1])
            width = D // blocks
            for block in range(blocks):
                right = jnp.concatenate([refs[items[block]][...] for _, items in pairs], axis=0)
                made[index, :, width * block:width * block + width] = dot_tn(left, right).astype(bf16)
            for part, (keep, other) in enumerate(ways):
                parity = (8 * index + part) // 3 % 2

                @pl.when(core == parity)
                def _(keep=keep):
                    keep.start()

                @pl.when(core != parity)
                def _(other=other):
                    other.start()

    @pl.when(step == len(plan) - 1)
    def _():
        for keep, _ in copies:
            keep.wait()


def spec(shape, index):
    return pl.BlockSpec(shape, index)


def whole(shape):
    return pl.BlockSpec(shape, lambda j: (0,) * len(shape))


SCALAR = pl.BlockSpec(memory_space=pltpu.SMEM)


def shape_of(shape, dtype):
    return jax.ShapeDtypeStruct(shape, dtype)


def params():
    return pltpu.CompilerParams(dimension_semantics=("arbitrary",), vmem_limit_bytes=VMEM_BYTES)


def cost(flops, moved):
    return pl.CostEstimate(flops=int(flops), bytes_accessed=int(moved), transcendentals=0)


def attn_fwd(segment, live, tokens, mem, weights, vectors):
    block = spec((ROWS, COLS), lambda j: (0, j))
    return pl.pallas_call(
        attn_fwd_kernel,
        grid=(STEPS,),
        in_specs=[
            SCALAR, spec((SEG_LEN, D), lambda j: (segment, 0)), whole((PADM, D)),
            spec((D, COLS), lambda j: (0, j)), spec((D, COLS), lambda j: (1, j)), spec((D, COLS), lambda j: (2, j)),
            spec((12, COLS), lambda j: (0, j)),
        ],
        out_specs=[whole((ROWS, D)), block, block, block, whole((16, ROWS_LANES)), block],
        out_shape=[shape_of((ROWS, D), bf16)] * 4 + [shape_of((16, ROWS_LANES), f32), shape_of((ROWS, D), bf16)],
        scratch_shapes=[pltpu.VMEM((ROWS_LANES, 128), f32)],
        compiler_params=params(),
        name="attn_fwd",
        cost_estimate=cost(5e9, 8e6),
    )(live, tokens, mem, weights, weights, weights, vectors)


def ffn_fwd(segment, live, tokens, mem, attended, weights, vectors, output):
    full = whole((ROWS, D))
    chunk = spec((ROWS, D), lambda j: (0, j))
    col = whole((ROWS, 1))
    return pl.pallas_call(
        ffn_fwd_kernel,
        grid=(CHUNKS,),
        in_specs=[
            SCALAR, spec((SEG_LEN, D), lambda j: (segment, 0)), whole((PADM, D)), full,
            spec((D, D), lambda j: (3, 0)), spec((D, D), lambda j: (4 + j, 0)), spec((D, D), lambda j: (8 + j, 0)),
            whole((12, D)),
        ] + [pl.BlockSpec(memory_space=pl.ANY)] * (output is not None),
        out_specs=[full, col, full, chunk, chunk, full, col, spec((SEG_LEN, D), lambda j: (segment, 0)), whole((PADM, D))],
        out_shape=[
            shape_of((ROWS, D), bf16), shape_of((ROWS, 1), f32), shape_of((ROWS, D), bf16), shape_of((ROWS, FF), bf16),
            shape_of((ROWS, FF), bf16), shape_of((ROWS, D), bf16), shape_of((ROWS, 1), f32),
            shape_of((SEGS * SEG_LEN, D), f32), shape_of((PADM, D), f32),
        ],
        input_output_aliases={} if output is None else {8: 7},
        scratch_shapes=[pltpu.VMEM((ROWS, D), f32)] * 2,
        compiler_params=params(),
        name="ffn_fwd",
        cost_estimate=cost(6e9, 25e6),
    )(live, tokens, mem, attended, weights, weights, weights, vectors, *([] if output is None else [output]))


def ffn_bwd(segment, live, cotangent, dmem, saved, weights, vectors):
    n1, i1, h1b, g, slope, n2, i2 = saved
    full = whole((ROWS, D))
    chunk = spec((ROWS, D), lambda j: (0, j))
    col = whole((ROWS, 1))
    return pl.pallas_call(
        ffn_bwd_kernel,
        grid=(CHUNKS,),
        in_specs=[
            SCALAR, spec((SEG_LEN, D), lambda j: (segment, 0)), whole((PADM, D)), full, col, full, col, chunk,
            spec((D, D), lambda j: (3, 0)), spec((D, D), lambda j: (4 + j, 0)), spec((D, D), lambda j: (8 + j, 0)),
            whole((12, D)),
        ],
        out_specs=[full, chunk, full, full, full, whole((12, D))],
        out_shape=[
            shape_of((ROWS, D), bf16), shape_of((ROWS, FF), bf16), shape_of((ROWS, D), bf16),
            shape_of((ROWS, D), f32), shape_of((ROWS, D), bf16), shape_of((12, D), f32),
        ],
        scratch_shapes=[pltpu.VMEM((ROWS, D), f32)],
        compiler_params=params(),
        name="ffn_bwd",
        cost_estimate=cost(6e9, 25e6),
    )(live, cotangent, dmem, n1, i1, n2, i2, slope, weights, weights, weights, vectors)


def attn_bwd(first, steps, live, q, k, v, da, lse, du, weights):
    block = spec((ROWS, COLS), lambda j: (0, first + j))
    own = spec((ROWS, COLS), lambda j: (0, j))
    return pl.pallas_call(
        functools.partial(attn_bwd_kernel, first),
        grid=(steps,),
        in_specs=[
            SCALAR, block, block, block, block, whole((16, ROWS_LANES)), whole((ROWS, D)),
            spec((D, COLS), lambda j: (0, first + j)), spec((D, COLS), lambda j: (1, first + j)),
            spec((D, COLS), lambda j: (2, first + j)),
        ],
        out_specs=[own, own, own, spec((8, COLS), lambda j: (0, j)), whole((ROWS, D))],
        out_shape=[shape_of((ROWS, steps * COLS), bf16)] * 3 + [
            shape_of((8, steps * COLS), f32), shape_of((ROWS, D), f32)],
        compiler_params=params(),
        name="attn_bwd",
        cost_estimate=cost(4e9, 5e6),
    )(live, q, k, v, da, lse, du, weights, weights, weights)


def grad_piece(products, name):
    arrays, specs, plan = [], [], []

    def add(array, chunk, width):
        for index, (have, *at) in enumerate(arrays):
            if have is array and at == [chunk, width]:
                return index
        arrays.append((array, chunk, width))
        specs.append(spec((ROWS, width), lambda j: (0, chunk)))
        return len(arrays) - 1

    def add_right(right):
        return [add(*part, COLS) for part in right] if isinstance(right, list) else [add(right, 0, D)]

    for lefts, chunk, rights in products:
        plan.append([(add(left, chunk, D), add_right(right)) for left, right in zip(lefts, rights)])
    anywhere = pl.BlockSpec(memory_space=pl.ANY)
    return pl.pallas_call(
        functools.partial(grad_kernel, plan, len(arrays)),
        grid=(len(plan),),
        in_specs=[SCALAR] + specs,
        out_specs=[anywhere] * 2,
        out_shape=[shape_of((4, 288, D), bf16)] * 2,
        scratch_shapes=[pltpu.VMEM((3, D, D), bf16), pltpu.SemaphoreType.DMA((3, 8))],
        compiler_params=params(),
        name=name,
        cost_estimate=cost(4e9, 15e6),
    )(rank_bits(), *[item[0] for item in arrays])


BITS = ("y", "x", "z1", "z0", "c")


def rank_bits():
    place, line = lax.axis_index("dp"), lax.axis_index("fsdp")
    return jnp.stack([place // 2 % 2, place % 2, line // 4 % 2, line // 2 % 2, line % 2]).astype(jnp.int32)


STRIDE = {"y": 16, "x": 8, "z1": 4, "z0": 2, "c": 1}


def swap(value, dims):
    mask = sum(STRIDE[dim] for dim in dims)
    return lax.ppermute(value, ("dp", "fsdp"), [(d, d ^ mask) for d in range(32)])


def add_low(left, right):
    return (left.astype(f32) + right.astype(f32)).astype(bf16)


class Part:
    def __init__(self, keeps, gots, names, dim, split=False):
        self.keeps, self.gots, self.names, self.dim, self.split = keeps, gots, names, dim, split


def columns(items):
    cut = [array[..., block * size:(block + 1) * size] for array, block, size in items]
    return cut[0] if len(cut) == 1 else jnp.concatenate(cut, axis=-1)


def combine(*parts):
    made = []
    for part in parts:
        keep, got = columns(part.keeps), columns(part.gots)
        if part.dim is None:
            made.append(add_low(keep, got))
            continue
        axis = part.names.index(part.dim)
        bit = rank_bits()[BITS.index(part.dim)]
        stays, goes = (
            add_low(*(lax.dynamic_index_in_dim(item, at, axis, keepdims=False) for item in (keep, got)))
            for at in (bit, 1 - bit))
        made.append(stays)
        width = goes.shape[-1] // 2
        made += [goes[..., :width], goes[..., width:]] if part.split else [goes]
    return made


def row_major(array):
    return with_layout_constraint(array, Layout(major_to_minor=tuple(range(array.ndim))))


def exchange(run, values, *sends):
    flat, tree = jax.tree.flatten((values, [array for array, _ in sends]))
    values, arrays = jax.tree.unflatten(tree, lax.optimization_barrier(tuple(flat)))
    arrays = [row_major(array) for array in arrays]
    gots = [row_major(swap(array, (dim,))) for array, (_, dim) in zip(arrays, sends)]
    flat, tree = jax.tree.flatten((run(values), gots))
    result, gots = jax.tree.unflatten(tree, lax.optimization_barrier(tuple(flat)))
    return (result,) + tuple(gots)


def unsplit(pair, parity):
    keep, other = pair
    even, odd = jnp.where(parity == 0, keep, other), jnp.where(parity == 0, other, keep)
    return jnp.stack([even, odd], axis=1).reshape(-1, D)


def column_blocks(parts, index):
    return [(part[index], j) for part in parts for j in range(part[index].shape[1] // COLS)]


def spread(own):
    place = lax.axis_index("dp")
    arrived = []
    for mask, dims in enumerate(((), ("x",), ("y",), ("x", "y"))):
        block = lax.dynamic_index_in_dim(own, place ^ mask, 0, keepdims=False)
        arrived.append(swap(block, dims) if dims else block)
    quarters = jnp.stack(arrived).reshape((2, 2) + arrived[0].shape)
    quarters = jnp.where(place // 2 == 1, quarters[::-1], quarters)
    quarters = jnp.where(place % 2 == 1, quarters[:, ::-1], quarters)
    return quarters.reshape(-1, D).astype(f32)


def adam_update(parameter, gradient, moment_one, moment_two, decay_factor):
    new_one = beta_one * moment_one + (1.0 - beta_one) * gradient
    new_two = beta_two * moment_two + (1.0 - beta_two) * gradient * gradient
    corrected_one = new_one / (1.0 - beta_one**adam_step)
    corrected_two = new_two / (1.0 - beta_two**adam_step)
    update = corrected_one / (jnp.sqrt(corrected_two) + adam_eps) + decay_factor * parameter
    return (update, new_one, new_two)


def local_grads(tokens, memory_init, chain_tokens, cotangent, weights, vectors):
    mem = jnp.pad(memory_init, ((0, PADM - MEM), (0, 0)))
    lives = [jnp.clip(chain_tokens - s * SEG_LEN, 0, SEG_LEN) for s in range(SEGS)]
    kept = []
    out = None
    for s in range(SEGS):
        x, q, k, v, lse, a = attn_fwd(s, lives[s], tokens, mem, weights, vectors)
        *saved, out, mem = ffn_fwd(s, lives[s], tokens, mem, a, weights, vectors, out)
        kept.append((x, q, k, v, lse, a, saved))
    dmem = jnp.zeros((PADM, D), f32)
    back = [None] * SEGS
    token_grads = [None] * SEGS
    pick = lambda items, i: [item[i] for item in items]
    x, a = pick(kept, 0), pick(kept, 5)
    h, g = ([k_[6][i] for k_ in kept] for i in (2, 3))
    custom = (lax.axis_size("dp"), lax.axis_size("fsdp")) == (4, 8)
    custom = (lax.axis_size("dp"), lax.axis_size("fsdp")) == (4, 8)
    for s in reversed(range(SEGS)):
        _, q, k, v, lse, _, saved = kept[s]
        dfb, dzb, dob, du, da, sums = ffn_bwd(s, lives[s], cotangent, dmem, saved, weights, vectors)
        back[s] = (dfb, dzb, dob, sums)
        parts = []

        def attend(state, steps=1, s=s, parts=parts):
            *part, out = attn_bwd(len(parts), steps, lives[s], *kept[s][1:4], *state, weights)
            parts.append(part)
            return (state[0], state[1], out)

        state = (da, lse, du)
        if s > 0:
            state = attend(state, STEPS)
            back[s] += (parts,)
        else:
            df, dz, do = (pick(back, i) for i in range(3))
            run_down = lambda df: grad_piece([(g, 1, df), (g, 2, df), (g, 3, df)], "grad_down")
            run_mixed = lambda dz: grad_piece([(dz, 2, h), (dz, 3, h), (g, 0, df)], "grad_mixed")
            run_up = lambda do: grad_piece([(a, 0, do), (dz, 0, h), (dz, 1, h)], "grad_up")
            back[0] += (parts,)
            run_qkv = lambda x: grad_piece(
                [(x, 0, [column_blocks(item[4], i) for item in back]) for i in range(3)], "grad_qkv")
            down = run_down(df)
            if not custom:
                mixed, up = run_mixed(dz), run_up(do)
                for _ in range(STEPS):
                    state = attend(state)
            else:
                full = lambda *items: [(item, 0, item.shape[-1]) for item in items]
                view = lambda item: item.reshape((2,) * 4 + (72, D))
                plane = ["z1", "z0", "y", "x"]
                d_keep, d_send = map(view, down)
                mixed, d_got = exchange(run_mixed, dz, (d_send, "c"))
                d_keep, d_left, d_right = combine(Part(full(d_keep), full(d_got), plane, "x", True))
                m_keep, m_send = map(view, mixed)
                up, d_got, m_got = exchange(run_up, do, (d_left, "x"), (m_send, "c"))
                m_keep, m_left, m_right = combine(Part(full(m_keep), full(m_got), plane, "z0", True))
                u_keep, u_send = map(view, up)
                state, d_more, m_got, u_got = exchange(attend, state, (d_right, "x"), (m_left, "z0"), (u_send, "c"))
                d_keep, d_send, u_keep, u_left, u_right = combine(
                    Part(full(d_keep), full(d_got, d_more), ["z1", "z0", "y"], "y"),
                    Part(full(u_keep), full(u_got), plane, "x", True))
                state, d_got, m_more, u_got = exchange(attend, state, (d_send, "y"), (m_right, "z0"), (u_left, "x"))
                d_keep, d_send, m_keep, m_send = combine(
                    Part(full(d_keep), full(d_got), ["z1", "z0"], "z0"),
                    Part(full(m_keep), full(m_got, m_more), ["z1", "y", "x"], "y"))
                state, d_got, m_got, u_more = exchange(attend, state, (d_send, "z0"), (m_send, "y"), (u_right, "x"))
                d_keep, d_send, m_keep, m_send, u_keep, u_send = combine(
                    Part(full(d_keep), full(d_got), ["z1"], "z1"),
                    Part(full(m_keep), full(m_got), ["z1", "x"], "x"),
                    Part(full(u_keep), full(u_got, u_more), ["z1", "z0", "y"], "y"))
        du = state[2]
        token_grads[s] = du[:SEG_LEN]
        dmem = du[SEG_LEN:SEG_LEN + PADM] + du[SEG_LEN + PADM:] + jnp.where(lives[s] > 0, 0.0, dmem)
    sums = sum(pick(back, 3))
    sums_qv = sum(jnp.concatenate([part[3] for part in item[4]], axis=1) for item in back)
    small = jnp.concatenate([sums_qv[0:2], sums[2:], dmem[:MEM]], axis=0)
    if custom:
        plus = lambda dim: (lambda value: value + swap(value, (dim,)))
        (triple, small), d_got, m_got, u_got = exchange(
            lambda both: (run_qkv(both[0]), plus("c")(both[1])), (x, small),
            (d_send, "z1"), (m_send, "x"), (u_send, "y"))
        m_keep, m_send, u_keep, u_send = combine(
            Part(full(m_keep), full(m_got), ["z1"], "z1"), Part(full(u_keep), full(u_got), ["z1", "z0"], "z0"))
        t_keep, t_send = map(view, triple)
        small, t_got = exchange(plus("z0"), small, (t_send, "c"))
        halves = lambda item: [[(item, i, D // 2)] for i in range(2)]
        (k0, k1), (g0, g1) = halves(t_keep), halves(t_got)
        k0, s0, k1, s1 = combine(Part(k0, g0, plane, "x"), Part(k1, g1, plane, "y"))
        small, g0, g1, u_got = exchange(plus("z1"), small, (s0, "x"), (s1, "y"), (u_send, "z0"))
        k0, s0, k1, s1, u_keep, u_send = combine(
            Part(full(k0), full(g0), ["z1", "z0", "y"], "y"), Part(full(k1), full(g1), ["z1", "z0", "x"], "x"),
            Part(full(u_keep), full(u_got), ["z1"], "z1"))
        _, g0, g1, u_got = exchange(lambda value: value, (), (s0, "y"), (s1, "x"), (u_send, "z1"))
        t_keep, t_send = combine(Part(full(k0, k1), full(g0, g1), ["z1", "z0"], "z0"))
        small, t_got, m_got = exchange(plus("x"), small, (t_send, "z0"), (m_send, "z1"))
        t_keep, t_send = combine(Part(full(t_keep), full(t_got), ["z1"], "z1"))
        small, t_got = exchange(plus("y"), small, (t_send, "z1"))
        own = combine(*(Part(full(k), full(g), [], None) for k, g in (
            (t_keep, t_got), (u_keep, u_got), (m_keep, m_got), (d_keep, d_got))))
        weight_sum = spread(jnp.stack(own))
    else:
        parity = lax.axis_index("fsdp") % 2
        total = jnp.concatenate([unsplit(item, parity) for item in (run_qkv(x), up, mixed, down)], axis=0)
        weight_sum = lax.psum_scatter(total, ("dp", "fsdp"), scatter_dimension=0, tiled=True).astype(f32)
        small = lax.psum(small, ("dp", "fsdp"))
    return (out, jnp.concatenate(token_grads, 0), weight_sum, small)


def shards(
    tokens, memory_init, chain_tokens, cotangent, weights, weight_first, weight_second,
    vectors, vector_first, vector_second,
):
    axes = ("dp", "fsdp")
    total_chains = tokens.shape[0] * lax.axis_size(axes)
    grad_scale = float(total_chains * SEGS * SEG_LEN) ** (-0.5)
    gathered = lax.all_gather(weights.astype(bf16), axes, axis=0, tiled=True)
    output, token_grad, weight_sum, small = local_grads(
        tokens[0], memory_init, chain_tokens, cotangent[0], gathered, vectors)
    vector_sum, memory_sum = small[:-MEM], small[-MEM:]
    weight_grad = weight_sum * grad_scale
    vector_grad = vector_sum * grad_scale
    memory_grad = memory_sum * grad_scale
    weight_step, new_weight_first, new_weight_second = adam_update(
        weights, weight_grad, weight_first, weight_second, decay_rate)
    vector_step, new_vector_first, new_vector_second = adam_update(
        vectors, vector_grad, vector_first, vector_second, 0.0)
    return (
        output[None], token_grad[None], memory_grad, weight_grad, weight_step, new_weight_first, new_weight_second,
        vector_grad, vector_step, new_vector_first, new_vector_second,
    )


def solution(mesh):
    both = ("dp", "fsdp")
    chain = P(both, None, None)
    rows = P(both, None)
    return jax.shard_map(
        shards,
        mesh=mesh,
        in_specs=(chain, P(), P(both), chain, rows, rows, rows, P(), P(), P()),
        out_specs=(chain, chain, P(), rows, rows, rows, rows, P(), P(), P(), P()),
        check_vma=False,
    )
```

```python
import functools

import jax
import jax.numpy as jnp
from jax import lax
from jax.experimental import pallas as pl
from jax.experimental.layout import Layout, with_layout_constraint
from jax.experimental.pallas import tpu as pltpu
from jax.sharding import PartitionSpec as P

D = 768
HEADS = 12
HEAD = 64
FF = 3072
MEM = 10
SEG_LEN = 512
SEGS = 2
PADM = 16
ROWS = SEG_LEN + 2 * PADM
ROWS_LANES = -(-ROWS // 128) * 128
COLS = 256
STEPS = D // COLS
CHUNKS = FF // D

eps_norm = 1e-12
beta_one = 0.9
beta_two = 0.95
decay_rate = 0.1
adam_eps = 1e-08
adam_step = 10
neg_large = -1e30
LOG2E = 1.4426950408889634
SCORE2 = HEAD ** (-0.5) * LOG2E
ROOT = HEAD ** (-0.5)
f32 = jnp.float32
bf16 = jnp.bfloat16
VMEM_BYTES = 56 * 1024 * 1024


def dot_nn(left, right):
    return lax.dot_general(left, right, (((1,), (0,)), ((), ())), preferred_element_type=f32)


def dot_nt(left, right):
    return lax.dot_general(left, right, (((1,), (1,)), ((), ())), preferred_element_type=f32)


def dot_tn(left, right):
    return lax.dot_general(left, right, (((0,), (0,)), ((), ())), preferred_element_type=f32)


def valid_positions(shape, axis, live):
    at = lax.broadcasted_iota(jnp.int32, shape, axis)
    read = (at >= SEG_LEN) & (at < SEG_LEN + MEM)
    write = (at >= SEG_LEN + PADM) & (at < SEG_LEN + PADM + MEM)
    return (at < live) | read | write


def mask_half(values, half):
    lane = lax.broadcasted_iota(jnp.int32, values.shape, 1)
    keep = (lane < HEAD) if half == 0 else (lane >= HEAD)
    return jnp.where(keep, values, jnp.zeros_like(values))


def norm_rows(values):
    centred = values - jnp.mean(values, axis=-1, keepdims=True)
    inverse = lax.rsqrt(jnp.mean(centred * centred, axis=-1, keepdims=True) + eps_norm)
    return centred * inverse, inverse


def norm_back(gradient, normed, inverse, gain_row):
    scaled = gradient * gain_row
    centred = scaled - jnp.mean(scaled, axis=-1, keepdims=True)
    return inverse * (centred - normed * jnp.mean(scaled * normed, axis=-1, keepdims=True))


def gelu_parts(z):
    phi = 0.5 + 0.5 * lax.erf(z * 0.7071067811865476)
    return z * phi, phi + z * jnp.exp2(z * z * (-0.5 * LOG2E)) * 0.3989422804014327


def attn_fwd_kernel(
    live_ref, tok_ref, mem_ref, wq_ref, wk_ref, wv_ref, vec_ref,
    x_ref, q_ref, k_ref, v_ref, lse_ref, a_ref, lse_acc,
):
    step = pl.program_id(0)
    live = live_ref[0]

    @pl.when(step == 0)
    def _():
        x_ref[0:SEG_LEN] = tok_ref[...]
        low = mem_ref[...].astype(bf16)
        x_ref[SEG_LEN:SEG_LEN + PADM] = low
        x_ref[SEG_LEN + PADM:ROWS] = low
        lse_acc[...] = jnp.zeros_like(lse_acc)

    x = x_ref[...]
    q = (dot_nn(x, wq_ref[...]) + vec_ref[0:1]).astype(bf16)
    k = dot_nn(x, wk_ref[...]).astype(bf16)
    v = (dot_nn(x, wv_ref[...]) + vec_ref[1:2]).astype(bf16)
    q_ref[...] = q
    k_ref[...] = k
    v_ref[...] = v
    valid = valid_positions((1, ROWS), 1, live)
    lane = lax.broadcasted_iota(jnp.int32, (1, 128), 1)
    lse_all = lse_acc[0:ROWS]
    for pair in range(COLS // 128):
        cols = slice(128 * pair, 128 * pair + 128)
        qp, kp, vp = q[:, cols], k[:, cols], v[:, cols]
        total = None
        for half in range(2):
            s = dot_nt(qp, mask_half(kp, half))
            s = jnp.where(valid, s, neg_large)
            top = jnp.max(s, axis=1, keepdims=True)
            e = jnp.exp2((s - top) * SCORE2)
            amount = jnp.sum(e, axis=1, keepdims=True)
            p = (e * (1.0 / amount)).astype(bf16)
            lse = top * SCORE2 + jnp.log(amount) * LOG2E
            head = step * (COLS // HEAD) + 2 * pair + half
            lse_all = jnp.where(lane == head, lse, lse_all)
            part = dot_nn(p, mask_half(vp, half))
            total = part if total is None else total + part
        a_ref[:, cols] = total.astype(bf16)
    lse_acc[0:ROWS] = lse_all

    @pl.when(step == STEPS - 1)
    def _():
        lse_ref[...] = lse_acc[...].T[0:16]


def ffn_fwd_kernel(
    live_ref, tok_ref, mem_ref, a_ref, wo_ref, wu_ref, wd_ref, vec_ref, *refs,
):
    n1_ref, i1_ref, h1b_ref, g_ref, slope_ref, n2_ref, i2_ref, out_ref, next_ref, h1, acc = refs[-11:]
    step = pl.program_id(0)
    live = live_ref[0]

    @pl.when(step == 0)
    def _():
        branch = dot_nn(a_ref[...], wo_ref[...]) + vec_ref[2:3]
        mem = mem_ref[...]
        u = jnp.concatenate([tok_ref[...].astype(f32), mem, mem], axis=0)
        normed, inverse = norm_rows(u + branch)
        n1_ref[...] = normed.astype(bf16)
        i1_ref[...] = inverse
        full = normed * vec_ref[3:4] + vec_ref[4:5]
        h1[...] = full
        h1b_ref[...] = full.astype(bf16)
        acc[...] = full + vec_ref[5:6]

    bias = vec_ref[pl.ds(8 + step, 1), :]
    blocks = [slice(272 * i, 272 * i + 272) for i in range(2)]
    ahead = dot_nt(h1b_ref[blocks[0]], wu_ref[...]) + bias
    for index, rows in enumerate(blocks):
        z = ahead
        if index + 1 < len(blocks):
            ahead = dot_nt(h1b_ref[blocks[index + 1]], wu_ref[...]) + bias
        g, slope = gelu_parts(z)
        g = g.astype(bf16)
        g_ref[rows] = g
        slope_ref[rows] = slope.astype(bf16)
        acc[rows] += dot_nn(g, wd_ref[...])

    @pl.when(step == CHUNKS - 1)
    def _():
        normed, inverse = norm_rows(acc[...])
        n2_ref[...] = normed.astype(bf16)
        i2_ref[...] = inverse
        y = normed * vec_ref[6:7] + vec_ref[7:8]
        row = lax.broadcasted_iota(jnp.int32, (SEG_LEN, 1), 0)
        out_ref[...] = jnp.where(row < live, y[0:SEG_LEN], 0.0)
        next_ref[...] = jnp.where(live > 0, y[SEG_LEN + PADM:ROWS], mem_ref[...])


def ffn_bwd_kernel(
    live_ref, cot_ref, dmem_ref, n1_ref, i1_ref, n2_ref, i2_ref, slope_ref, wo_ref, wu_ref, wd_ref, vec_ref,
    dfb_ref, dzb_ref, dob_ref, dr1_ref, da_ref, sums_ref,
    acc,
):
    step = pl.program_id(0)
    live = live_ref[0]

    @pl.when(step == 0)
    def _():
        row = lax.broadcasted_iota(jnp.int32, (SEG_LEN, 1), 0)
        token = jnp.where(row < live, cot_ref[...].astype(f32), 0.0)
        write = jnp.where(live > 0, dmem_ref[...], 0.0)
        dy = jnp.concatenate([token, jnp.zeros((PADM, D), f32), write], axis=0)
        normed = n2_ref[...].astype(f32)
        sums_ref[...] = jnp.zeros_like(sums_ref)
        sums_ref[6:7] = jnp.sum(dy * normed, axis=0, keepdims=True)
        sums_ref[7:8] = jnp.sum(dy, axis=0, keepdims=True)
        back = norm_back(dy, normed, i2_ref[...], vec_ref[6:7])
        low = back.astype(bf16)
        dfb_ref[...] = low
        sums_ref[5:6] = jnp.sum(low.astype(f32), axis=0, keepdims=True)
        acc[...] = back

    blocks = [slice(ROWS // 2 * i, ROWS // 2 * (i + 1)) for i in range(2)]
    ahead = dot_nt(dfb_ref[blocks[0]], wd_ref[...])
    total = None
    for index, rows in enumerate(blocks):
        dg = ahead
        if index + 1 < len(blocks):
            ahead = dot_nt(dfb_ref[blocks[index + 1]], wd_ref[...])
        dz = (dg * slope_ref[rows].astype(f32)).astype(bf16)
        dzb_ref[rows] = dz
        part = jnp.sum(dz.astype(f32), axis=0, keepdims=True)
        total = part if total is None else total + part
        acc[rows] += dot_nn(dz, wu_ref[...])
    sums_ref[pl.ds(8 + step, 1), :] = total

    @pl.when(step == CHUNKS - 1)
    def _():
        dh = acc[...]
        normed = n1_ref[...].astype(f32)
        sums_ref[3:4] = jnp.sum(dh * normed, axis=0, keepdims=True)
        sums_ref[4:5] = jnp.sum(dh, axis=0, keepdims=True)
        back = norm_back(dh, normed, i1_ref[...], vec_ref[3:4])
        dr1_ref[...] = back
        low = back.astype(bf16)
        dob_ref[...] = low
        sums_ref[2:3] = jnp.sum(low.astype(f32), axis=0, keepdims=True)
        da_ref[...] = dot_nt(low, wo_ref[...]).astype(bf16)


def attn_bwd_kernel(
    first, outs, live_ref, q_ref, k_ref, v_ref, da_ref, lse_ref, dr1_ref, wq_ref, wk_ref, wv_ref, *refs,
):
    dq_ref, dk_ref, dv_ref, sums_ref, du_ref, *token_refs = refs[-outs:]
    live = live_ref[0]
    step = first + pl.program_id(0)

    @pl.when(step == first)
    def _():
        du_ref[...] = dr1_ref[...]

    valid = valid_positions((ROWS, 1), 0, live)
    for pair in range(COLS // 128):
        cols = slice(128 * pair, 128 * pair + 128)
        qp, kp, vp, dap = q_ref[:, cols], k_ref[:, cols], v_ref[:, cols], da_ref[:, cols]
        dq = dk = dv = None
        for half in range(2):
            head = step * (COLS // HEAD) + 2 * pair + half
            kh, vh, qh, dah = (mask_half(t, half) for t in (kp, vp, qp, dap))
            s = dot_nt(kh, qp)
            s = jnp.where(valid, s, neg_large)
            p = jnp.exp2(s * SCORE2 - lse_ref[pl.ds(head, 1), 0:ROWS])
            dp = dot_nt(vh, dap)
            inner = jnp.sum(p * dp, axis=0, keepdims=True)
            ds = (p * (dp - inner)).astype(bf16)
            parts = (dot_tn(ds, kh), dot_nn(ds, qh), dot_nn(p.astype(bf16), dah))
            if dq is None:
                dq, dk, dv = parts
            else:
                dq, dk, dv = dq + parts[0], dk + parts[1], dv + parts[2]
        dq_ref[:, cols] = (dq * ROOT).astype(bf16)
        dk_ref[:, cols] = (dk * ROOT).astype(bf16)
        dv_ref[:, cols] = dv.astype(bf16)
    dq, dk, dv = dq_ref[...], dk_ref[...], dv_ref[...]
    sums_ref[0:1] = jnp.sum(dq.astype(f32), axis=0, keepdims=True)
    sums_ref[1:2] = jnp.sum(dv.astype(f32), axis=0, keepdims=True)
    du_ref[...] += dot_nt(dq, wq_ref[...]) + dot_nt(dk, wk_ref[...]) + dot_nt(dv, wv_ref[...])
    for token_ref in token_refs:
        @pl.when(step == STEPS - 1)
        def _(token_ref=token_ref):
            token_ref[...] = du_ref[0:SEG_LEN]


def grad_kernel(plan, count, bits_ref, *refs):
    keep_ref, other_ref, made, sems = refs[count:]
    step = pl.program_id(0)
    core = bits_ref[BITS.index("c")]
    copies = []
    for index, pairs in enumerate(plan):
        ways = []
        for part in range(8):
            shard, third = divmod(8 * index + part, 3)
            source = made.at[index, pl.ds(96 * part, 96)]
            ways.append([
                pltpu.make_async_copy(source, target.at[shard // 2, pl.ds(96 * third, 96)], sems.at[index, part])
                for target in (keep_ref, other_ref)
            ])
        copies += ways

        @pl.when(step == index)
        def _(pairs=pairs, index=index, ways=ways):
            left = jnp.concatenate([refs[item][...] for item, _ in pairs], axis=0)
            blocks = len(pairs[0][1])
            width = D // blocks
            for block in range(blocks):
                right = jnp.concatenate([refs[items[block]][...] for _, items in pairs], axis=0)
                made[index, :, width * block:width * block + width] = dot_tn(left, right).astype(bf16)
            for part, (keep, other) in enumerate(ways):
                parity = (8 * index + part) // 3 % 2

                @pl.when(core == parity)
                def _(keep=keep):
                    keep.start()

                @pl.when(core != parity)
                def _(other=other):
                    other.start()

    @pl.when(step == len(plan) - 1)
    def _():
        for keep, _ in copies:
            keep.wait()


def spec(shape, index):
    return pl.BlockSpec(shape, index)


def whole(shape):
    return pl.BlockSpec(shape, lambda j: (0,) * len(shape))


SCALAR = pl.BlockSpec(memory_space=pltpu.SMEM)


def shape_of(shape, dtype):
    return jax.ShapeDtypeStruct(shape, dtype)


def params():
    return pltpu.CompilerParams(dimension_semantics=("arbitrary",), vmem_limit_bytes=VMEM_BYTES)


def cost(flops, moved):
    return pl.CostEstimate(flops=int(flops), bytes_accessed=int(moved), transcendentals=0)


def attn_fwd(segment, live, tokens, mem, weights, vectors):
    block = spec((ROWS, COLS), lambda j: (0, j))
    return pl.pallas_call(
        attn_fwd_kernel,
        grid=(STEPS,),
        in_specs=[
            SCALAR, spec((SEG_LEN, D), lambda j: (segment, 0)), whole((PADM, D)),
            spec((D, COLS), lambda j: (0, j)), spec((D, COLS), lambda j: (1, j)), spec((D, COLS), lambda j: (2, j)),
            spec((12, COLS), lambda j: (0, j)),
        ],
        out_specs=[whole((ROWS, D)), block, block, block, whole((16, ROWS_LANES)), block],
        out_shape=[shape_of((ROWS, D), bf16)] * 4 + [shape_of((16, ROWS_LANES), f32), shape_of((ROWS, D), bf16)],
        scratch_shapes=[pltpu.VMEM((ROWS_LANES, 128), f32)],
        compiler_params=params(),
        name="attn_fwd",
        cost_estimate=cost(5e9, 8e6),
    )(live, tokens, mem, weights, weights, weights, vectors)


def ffn_fwd(segment, live, tokens, mem, attended, weights, vectors, output):
    full = whole((ROWS, D))
    chunk = spec((ROWS, D), lambda j: (0, j))
    col = whole((ROWS, 1))
    return pl.pallas_call(
        ffn_fwd_kernel,
        grid=(CHUNKS,),
        in_specs=[
            SCALAR, spec((SEG_LEN, D), lambda j: (segment, 0)), whole((PADM, D)), full,
            spec((D, D), lambda j: (3, 0)), spec((D, D), lambda j: (4 + j, 0)), spec((D, D), lambda j: (8 + j, 0)),
            whole((12, D)),
        ] + [pl.BlockSpec(memory_space=pl.ANY)] * (output is not None),
        out_specs=[full, col, full, chunk, chunk, full, col, spec((SEG_LEN, D), lambda j: (segment, 0)), whole((PADM, D))],
        out_shape=[
            shape_of((ROWS, D), bf16), shape_of((ROWS, 1), f32), shape_of((ROWS, D), bf16), shape_of((ROWS, FF), bf16),
            shape_of((ROWS, FF), bf16), shape_of((ROWS, D), bf16), shape_of((ROWS, 1), f32),
            shape_of((SEGS * SEG_LEN, D), f32), shape_of((PADM, D), f32),
        ],
        input_output_aliases={} if output is None else {8: 7},
        scratch_shapes=[pltpu.VMEM((ROWS, D), f32)] * 2,
        compiler_params=params(),
        name="ffn_fwd",
        cost_estimate=cost(6e9, 25e6),
    )(live, tokens, mem, attended, weights, weights, weights, vectors, *([] if output is None else [output]))


def ffn_bwd(segment, live, cotangent, dmem, saved, weights, vectors):
    n1, i1, h1b, g, slope, n2, i2 = saved
    full = whole((ROWS, D))
    chunk = spec((ROWS, D), lambda j: (0, j))
    col = whole((ROWS, 1))
    return pl.pallas_call(
        ffn_bwd_kernel,
        grid=(CHUNKS,),
        in_specs=[
            SCALAR, spec((SEG_LEN, D), lambda j: (segment, 0)), whole((PADM, D)), full, col, full, col, chunk,
            spec((D, D), lambda j: (3, 0)), spec((D, D), lambda j: (4 + j, 0)), spec((D, D), lambda j: (8 + j, 0)),
            whole((12, D)),
        ],
        out_specs=[full, chunk, full, full, full, whole((12, D))],
        out_shape=[
            shape_of((ROWS, D), bf16), shape_of((ROWS, FF), bf16), shape_of((ROWS, D), bf16),
            shape_of((ROWS, D), f32), shape_of((ROWS, D), bf16), shape_of((12, D), f32),
        ],
        scratch_shapes=[pltpu.VMEM((ROWS, D), f32)],
        compiler_params=params(),
        name="ffn_bwd",
        cost_estimate=cost(6e9, 25e6),
    )(live, cotangent, dmem, n1, i1, n2, i2, slope, weights, weights, weights, vectors)


def attn_bwd(first, steps, segment, token_grad, live, q, k, v, da, lse, du, weights):
    block = spec((ROWS, COLS), lambda j: (0, first + j))
    own = spec((ROWS, COLS), lambda j: (0, j))
    last = first + steps == STEPS
    given = [token_grad] if last and token_grad is not None else []
    return pl.pallas_call(
        functools.partial(attn_bwd_kernel, first, 5 + last),
        grid=(steps,),
        in_specs=[
            SCALAR, block, block, block, block, whole((16, ROWS_LANES)), whole((ROWS, D)),
            spec((D, COLS), lambda j: (0, first + j)), spec((D, COLS), lambda j: (1, first + j)),
            spec((D, COLS), lambda j: (2, first + j)),
        ] + [pl.BlockSpec(memory_space=pl.ANY)] * len(given),
        out_specs=[own, own, own, spec((8, COLS), lambda j: (0, j)), whole((ROWS, D))]
        + [spec((SEG_LEN, D), lambda j: (segment, 0))] * last,
        out_shape=[shape_of((ROWS, steps * COLS), bf16)] * 3 + [
            shape_of((8, steps * COLS), f32), shape_of((ROWS, D), f32)]
        + [shape_of((SEGS * SEG_LEN, D), f32)] * last,
        input_output_aliases={10: 5} if given else {},
        compiler_params=params(),
        name="attn_bwd",
        cost_estimate=cost(4e9, 5e6),
    )(live, q, k, v, da, lse, du, weights, weights, weights, *given)


def grad_piece(products, name):
    arrays, specs, plan = [], [], []

    def add(array, chunk, width):
        for index, (have, *at) in enumerate(arrays):
            if have is array and at == [chunk, width]:
                return index
        arrays.append((array, chunk, width))
        specs.append(spec((ROWS, width), lambda j: (0, chunk)))
        return len(arrays) - 1

    def add_right(right):
        return [add(*part, COLS) for part in right] if isinstance(right, list) else [add(right, 0, D)]

    for lefts, chunk, rights in products:
        plan.append([(add(left, chunk, D), add_right(right)) for left, right in zip(lefts, rights)])
    anywhere = pl.BlockSpec(memory_space=pl.ANY)
    return pl.pallas_call(
        functools.partial(grad_kernel, plan, len(arrays)),
        grid=(len(plan),),
        in_specs=[SCALAR] + specs,
        out_specs=[anywhere] * 2,
        out_shape=[shape_of((4, 288, D), bf16)] * 2,
        scratch_shapes=[pltpu.VMEM((3, D, D), bf16), pltpu.SemaphoreType.DMA((3, 8))],
        compiler_params=params(),
        name=name,
        cost_estimate=cost(4e9, 15e6),
    )(rank_bits(), *[item[0] for item in arrays])


BITS = ("y", "x", "z1", "z0", "c")


def rank_bits():
    place, line = lax.axis_index("dp"), lax.axis_index("fsdp")
    return jnp.stack([place // 2 % 2, place % 2, line // 4 % 2, line // 2 % 2, line % 2]).astype(jnp.int32)


STRIDE = {"y": 16, "x": 8, "z1": 4, "z0": 2, "c": 1}


def swap(value, dims):
    mask = sum(STRIDE[dim] for dim in dims)
    return lax.ppermute(value, ("dp", "fsdp"), [(d, d ^ mask) for d in range(32)])


def add_low(left, right):
    return (left.astype(f32) + right.astype(f32)).astype(bf16)


class Part:
    def __init__(self, keeps, gots, names, dim, split=False):
        self.keeps, self.gots, self.names, self.dim, self.split = keeps, gots, names, dim, split


def columns(items):
    cut = [array[..., block * size:(block + 1) * size] for array, block, size in items]
    return cut[0] if len(cut) == 1 else jnp.concatenate(cut, axis=-1)


def combine(*parts):
    made = []
    for part in parts:
        keep, got = columns(part.keeps), columns(part.gots)
        if part.dim is None:
            made.append(add_low(keep, got))
            continue
        axis = part.names.index(part.dim)
        bit = rank_bits()[BITS.index(part.dim)]
        stays, goes = (
            add_low(*(lax.dynamic_index_in_dim(item, at, axis, keepdims=False) for item in (keep, got)))
            for at in (bit, 1 - bit))
        made.append(stays)
        width = goes.shape[-1] // 2
        made += [goes[..., :width], goes[..., width:]] if part.split else [goes]
    return made


def row_major(array):
    return with_layout_constraint(array, Layout(major_to_minor=tuple(range(array.ndim))))


def exchange(run, values, *sends):
    flat, tree = jax.tree.flatten((values, [array for array, _ in sends]))
    values, arrays = jax.tree.unflatten(tree, lax.optimization_barrier(tuple(flat)))
    arrays = [row_major(array) for array in arrays]
    gots = [row_major(swap(array, (dim,))) for array, (_, dim) in zip(arrays, sends)]
    flat, tree = jax.tree.flatten((run(values), gots))
    result, gots = jax.tree.unflatten(tree, lax.optimization_barrier(tuple(flat)))
    return (result,) + tuple(gots)


def unsplit(pair, parity):
    keep, other = pair
    even, odd = jnp.where(parity == 0, keep, other), jnp.where(parity == 0, other, keep)
    return jnp.stack([even, odd], axis=1).reshape(-1, D)


def column_blocks(parts, index):
    return [(part[index], j) for part in parts for j in range(part[index].shape[1] // COLS)]


def spread(own):
    place = lax.axis_index("dp")
    arrived = []
    for mask, dims in enumerate(((), ("x",), ("y",), ("x", "y"))):
        block = lax.dynamic_index_in_dim(own, place ^ mask, 0, keepdims=False)
        arrived.append(swap(block, dims) if dims else block)
    quarters = jnp.stack(arrived).reshape((2, 2) + arrived[0].shape)
    quarters = jnp.where(place // 2 == 1, quarters[::-1], quarters)
    quarters = jnp.where(place % 2 == 1, quarters[:, ::-1], quarters)
    return quarters.reshape(-1, D).astype(f32)


def adam_update(parameter, gradient, moment_one, moment_two, decay_factor):
    new_one = beta_one * moment_one + (1.0 - beta_one) * gradient
    new_two = beta_two * moment_two + (1.0 - beta_two) * gradient * gradient
    corrected_one = new_one / (1.0 - beta_one**adam_step)
    corrected_two = new_two / (1.0 - beta_two**adam_step)
    update = corrected_one / (jnp.sqrt(corrected_two) + adam_eps) + decay_factor * parameter
    return (update, new_one, new_two)


def local_grads(tokens, memory_init, chain_tokens, cotangent, weights, vectors):
    mem = jnp.pad(memory_init, ((0, PADM - MEM), (0, 0)))
    lives = [jnp.clip(chain_tokens - s * SEG_LEN, 0, SEG_LEN) for s in range(SEGS)]
    kept = []
    out = None
    for s in range(SEGS):
        x, q, k, v, lse, a = attn_fwd(s, lives[s], tokens, mem, weights, vectors)
        *saved, out, mem = ffn_fwd(s, lives[s], tokens, mem, a, weights, vectors, out)
        kept.append((x, q, k, v, lse, a, saved))
    dmem = jnp.zeros((PADM, D), f32)
    back = [None] * SEGS
    token_grad = None
    pick = lambda items, i: [item[i] for item in items]
    x, a = pick(kept, 0), pick(kept, 5)
    h, g = ([k_[6][i] for k_ in kept] for i in (2, 3))
    custom = (lax.axis_size("dp"), lax.axis_size("fsdp")) == (4, 8)
    custom = (lax.axis_size("dp"), lax.axis_size("fsdp")) == (4, 8)
    for s in reversed(range(SEGS)):
        _, q, k, v, lse, _, saved = kept[s]
        dfb, dzb, dob, du, da, sums = ffn_bwd(s, lives[s], cotangent, dmem, saved, weights, vectors)
        back[s] = (dfb, dzb, dob, sums)
        parts = []

        def attend(state, steps=1, s=s, parts=parts):
            *part, sums_qv, out = (made := attn_bwd(
                len(parts), steps, s, state[3], lives[s], *kept[s][1:4], *state[:3], weights))[:5]
            parts.append((*part, sums_qv))
            return (state[0], state[1], out, made[5] if len(made) > 5 else state[3])

        state = (da, lse, du, token_grad)
        if s > 0:
            state = attend(state, STEPS)
            back[s] += (parts,)
        else:
            df, dz, do = (pick(back, i) for i in range(3))
            run_down = lambda df: grad_piece([(g, 1, df), (g, 2, df), (g, 3, df)], "grad_down")
            run_mixed = lambda dz: grad_piece([(dz, 2, h), (dz, 3, h), (g, 0, df)], "grad_mixed")
            run_up = lambda do: grad_piece([(a, 0, do), (dz, 0, h), (dz, 1, h)], "grad_up")
            back[0] += (parts,)
            run_qkv = lambda x: grad_piece(
                [(x, 0, [column_blocks(item[4], i) for item in back]) for i in range(3)], "grad_qkv")
            down = run_down(df)
            if not custom:
                mixed, up = run_mixed(dz), run_up(do)
                for _ in range(STEPS):
                    state = attend(state)
            else:
                full = lambda *items: [(item, 0, item.shape[-1]) for item in items]
                view = lambda item: item.reshape((2,) * 4 + (72, D))
                plane = ["z1", "z0", "y", "x"]
                d_keep, d_send = map(view, down)
                mixed, d_got = exchange(run_mixed, dz, (d_send, "c"))
                d_keep, d_left, d_right = combine(Part(full(d_keep), full(d_got), plane, "x", True))
                m_keep, m_send = map(view, mixed)
                up, d_got, m_got = exchange(run_up, do, (d_left, "x"), (m_send, "c"))
                m_keep, m_left, m_right = combine(Part(full(m_keep), full(m_got), plane, "z0", True))
                u_keep, u_send = map(view, up)
                state, d_more, m_got, u_got = exchange(attend, state, (d_right, "x"), (m_left, "z0"), (u_send, "c"))
                d_keep, d_send, u_keep, u_left, u_right = combine(
                    Part(full(d_keep), full(d_got, d_more), ["z1", "z0", "y"], "y"),
                    Part(full(u_keep), full(u_got), plane, "x", True))
                state, d_got, m_more, u_got = exchange(attend, state, (d_send, "y"), (m_right, "z0"), (u_left, "x"))
                d_keep, d_send, m_keep, m_send = combine(
                    Part(full(d_keep), full(d_got), ["z1", "z0"], "z0"),
                    Part(full(m_keep), full(m_got, m_more), ["z1", "y", "x"], "y"))
                state, d_got, m_got, u_more = exchange(attend, state, (d_send, "z0"), (m_send, "y"), (u_right, "x"))
                d_keep, d_send, m_keep, m_send, u_keep, u_send = combine(
                    Part(full(d_keep), full(d_got), ["z1"], "z1"),
                    Part(full(m_keep), full(m_got), ["z1", "x"], "x"),
                    Part(full(u_keep), full(u_got, u_more), ["z1", "z0", "y"], "y"))
        du, token_grad = state[2:]
        dmem = du[SEG_LEN:SEG_LEN + PADM] + du[SEG_LEN + PADM:] + jnp.where(lives[s] > 0, 0.0, dmem)
    sums = sum(pick(back, 3))
    sums_qv = sum(jnp.concatenate([part[3] for part in item[4]], axis=1) for item in back)
    small = jnp.concatenate([sums_qv[0:2], sums[2:], dmem[:MEM]], axis=0)
    if custom:
        plus = lambda dim: (lambda value: value + swap(value, (dim,)))
        (triple, small), d_got, m_got, u_got = exchange(
            lambda both: (run_qkv(both[0]), plus("c")(both[1])), (x, small),
            (d_send, "z1"), (m_send, "x"), (u_send, "y"))
        m_keep, m_send, u_keep, u_send = combine(
            Part(full(m_keep), full(m_got), ["z1"], "z1"), Part(full(u_keep), full(u_got), ["z1", "z0"], "z0"))
        t_keep, t_send = map(view, triple)
        small, t_got = exchange(plus("z0"), small, (t_send, "c"))
        halves = lambda item: [[(item, i, D // 2)] for i in range(2)]
        (k0, k1), (g0, g1) = halves(t_keep), halves(t_got)
        k0, s0, k1, s1 = combine(Part(k0, g0, plane, "x"), Part(k1, g1, plane, "y"))
        small, g0, g1, u_got = exchange(plus("z1"), small, (s0, "x"), (s1, "y"), (u_send, "z0"))
        k0, s0, k1, s1, u_keep, u_send = combine(
            Part(full(k0), full(g0), ["z1", "z0", "y"], "y"), Part(full(k1), full(g1), ["z1", "z0", "x"], "x"),
            Part(full(u_keep), full(u_got), ["z1"], "z1"))
        _, g0, g1, u_got = exchange(lambda value: value, (), (s0, "y"), (s1, "x"), (u_send, "z1"))
        t_keep, t_send = combine(Part(full(k0, k1), full(g0, g1), ["z1", "z0"], "z0"))
        small, t_got, m_got = exchange(plus("x"), small, (t_send, "z0"), (m_send, "z1"))
        t_keep, t_send = combine(Part(full(t_keep), full(t_got), ["z1"], "z1"))
        small, t_got = exchange(plus("y"), small, (t_send, "z1"))
        own = combine(*(Part(full(k), full(g), [], None) for k, g in (
            (t_keep, t_got), (u_keep, u_got), (m_keep, m_got), (d_keep, d_got))))
        weight_sum = spread(jnp.stack(own))
    else:
        parity = lax.axis_index("fsdp") % 2
        total = jnp.concatenate([unsplit(item, parity) for item in (run_qkv(x), up, mixed, down)], axis=0)
        weight_sum = lax.psum_scatter(total, ("dp", "fsdp"), scatter_dimension=0, tiled=True).astype(f32)
        small = lax.psum(small, ("dp", "fsdp"))
    return (out, token_grad, weight_sum, small)


def shards(
    tokens, memory_init, chain_tokens, cotangent, weights, weight_first, weight_second,
    vectors, vector_first, vector_second,
):
    axes = ("dp", "fsdp")
    total_chains = tokens.shape[0] * lax.axis_size(axes)
    grad_scale = float(total_chains * SEGS * SEG_LEN) ** (-0.5)
    gathered = lax.all_gather(weights.astype(bf16), axes, axis=0, tiled=True)
    output, token_grad, weight_sum, small = local_grads(
        tokens[0], memory_init, chain_tokens, cotangent[0], gathered, vectors)
    vector_sum, memory_sum = small[:-MEM], small[-MEM:]
    weight_grad = weight_sum * grad_scale
    vector_grad = vector_sum * grad_scale
    memory_grad = memory_sum * grad_scale
    weight_step, new_weight_first, new_weight_second = adam_update(
        weights, weight_grad, weight_first, weight_second, decay_rate)
    vector_step, new_vector_first, new_vector_second = adam_update(
        vectors, vector_grad, vector_first, vector_second, 0.0)
    return (
        output[None], token_grad[None], memory_grad, weight_grad, weight_step, new_weight_first, new_weight_second,
        vector_grad, vector_step, new_vector_first, new_vector_second,
    )


def solution(mesh):
    both = ("dp", "fsdp")
    chain = P(both, None, None)
    rows = P(both, None)
    return jax.shard_map(
        shards,
        mesh=mesh,
        in_specs=(chain, P(), P(both), chain, rows, rows, rows, P(), P(), P()),
        out_specs=(chain, chain, P(), rows, rows, rows, rows, P(), P(), P(), P()),
        check_vma=False,
    )
```

```python
import functools

import jax
import jax.numpy as jnp
from jax import lax
from jax.experimental import pallas as pl
from jax.experimental.layout import Layout, with_layout_constraint
from jax.experimental.pallas import tpu as pltpu
from jax.sharding import PartitionSpec as P

D = 768
HEADS = 12
HEAD = 64
FF = 3072
MEM = 10
SEG_LEN = 512
SEGS = 2
PADM = 16
ROWS = SEG_LEN + 2 * PADM
ROWS_LANES = -(-ROWS // 128) * 128
COLS = 256
STEPS = D // COLS
CHUNKS = FF // D

eps_norm = 1e-12
beta_one = 0.9
beta_two = 0.95
decay_rate = 0.1
adam_eps = 1e-08
adam_step = 10
neg_large = -1e30
LOG2E = 1.4426950408889634
SCORE2 = HEAD ** (-0.5) * LOG2E
ROOT = HEAD ** (-0.5)
f32 = jnp.float32
bf16 = jnp.bfloat16
VMEM_BYTES = 56 * 1024 * 1024


def dot_nn(left, right):
    return lax.dot_general(left, right, (((1,), (0,)), ((), ())), preferred_element_type=f32)


def dot_nt(left, right):
    return lax.dot_general(left, right, (((1,), (1,)), ((), ())), preferred_element_type=f32)


def dot_tn(left, right):
    return lax.dot_general(left, right, (((0,), (0,)), ((), ())), preferred_element_type=f32)


def valid_positions(shape, axis, live):
    at = lax.broadcasted_iota(jnp.int32, shape, axis)
    read = (at >= SEG_LEN) & (at < SEG_LEN + MEM)
    write = (at >= SEG_LEN + PADM) & (at < SEG_LEN + PADM + MEM)
    return (at < live) | read | write


def mask_half(values, half):
    lane = lax.broadcasted_iota(jnp.int32, values.shape, 1)
    keep = (lane < HEAD) if half == 0 else (lane >= HEAD)
    return jnp.where(keep, values, jnp.zeros_like(values))


QUAD = COLS // HEAD
BLOCK = 272
MEMS = 2 * PADM


def stack_heads(values):
    tall = jnp.concatenate([values[SEG_LEN:]] * QUAD, axis=0)
    return jnp.where(own_lanes(tall.shape), tall, jnp.zeros_like(tall))


def own_lanes(shape):
    row = lax.broadcasted_iota(jnp.int32, shape, 0)
    lane = lax.broadcasted_iota(jnp.int32, shape, 1)
    return row // MEMS == lane // HEAD


def norm_rows(values):
    centred = values - jnp.mean(values, axis=-1, keepdims=True)
    inverse = lax.rsqrt(jnp.mean(centred * centred, axis=-1, keepdims=True) + eps_norm)
    return centred * inverse, inverse


def norm_back(gradient, normed, inverse, gain_row):
    scaled = gradient * gain_row
    centred = scaled - jnp.mean(scaled, axis=-1, keepdims=True)
    return inverse * (centred - normed * jnp.mean(scaled * normed, axis=-1, keepdims=True))


def gelu_parts(z):
    phi = 0.5 + 0.5 * lax.erf(z * 0.7071067811865476)
    return z * phi, phi + z * jnp.exp2(z * z * (-0.5 * LOG2E)) * 0.3989422804014327


def attn_fwd_kernel(
    live_ref, tok_ref, mem_ref, wq_ref, wk_ref, wv_ref, vec_ref,
    x_ref, q_ref, k_ref, v_ref, lse_ref, a_ref, lse_acc,
):
    step = pl.program_id(0)
    live = live_ref[0]

    @pl.when(step == 0)
    def _():
        x_ref[0:SEG_LEN] = tok_ref[...]
        low = mem_ref[...].astype(bf16)
        x_ref[SEG_LEN:SEG_LEN + PADM] = low
        x_ref[SEG_LEN + PADM:ROWS] = low
        lse_acc[...] = jnp.zeros_like(lse_acc)

    x = x_ref[...]
    q = (dot_nn(x, wq_ref[...]) + vec_ref[0:1]).astype(bf16)
    k = dot_nn(x, wk_ref[...]).astype(bf16)
    v = (dot_nn(x, wv_ref[...]) + vec_ref[1:2]).astype(bf16)
    q_ref[...] = q
    k_ref[...] = k
    v_ref[...] = v
    lane = lax.broadcasted_iota(jnp.int32, (1, 128), 1)
    mem_at = lane % MEMS
    mem_valid = (mem_at < MEM) | ((mem_at >= PADM) & (mem_at < PADM + MEM))
    s_mem = jnp.where(mem_valid, dot_nt(q, stack_heads(k)), neg_large)
    valid = lax.broadcasted_iota(jnp.int32, (1, SEG_LEN), 1) < live
    lse_all = lse_acc[0:ROWS]
    p_mem = jnp.zeros((ROWS, 128), f32)
    totals = []
    for pair in range(COLS // 128):
        cols = slice(128 * pair, 128 * pair + 128)
        qp, kp, vp = q[:, cols], k[0:SEG_LEN, cols], v[0:SEG_LEN, cols]
        total = None
        for half in range(2):
            mine = lane // MEMS == 2 * pair + half
            s_all = dot_nt(qp, mask_half(kp, half))
            head = step * QUAD + 2 * pair + half
            rows_p, rows_mem, rows_lse = [], [], []
            for low in range(0, ROWS, BLOCK):
                s = jnp.where(valid, s_all[low:low + BLOCK], neg_large)
                mem = s_mem[low:low + BLOCK]
                tiles = [s[:, 128 * i:128 * i + 128] for i in range(SEG_LEN // 128)]
                peak = functools.reduce(jnp.maximum, tiles + [jnp.where(mine, mem, neg_large)])
                top = jnp.max(peak, axis=1, keepdims=True) * SCORE2
                e = jnp.exp2(s * SCORE2 - top)
                e_mem = jnp.where(mine, jnp.exp2(mem * SCORE2 - top), 0.0)
                tiles = [e[:, 128 * i:128 * i + 128] for i in range(SEG_LEN // 128)]
                amount = jnp.sum(functools.reduce(jnp.add, tiles + [e_mem]), axis=1, keepdims=True)
                inverse = 1.0 / amount
                rows_p.append((e * inverse).astype(bf16))
                rows_mem.append(e_mem * inverse)
                rows_lse.append(top + jnp.log(amount) * LOG2E)
            p = jnp.concatenate(rows_p, axis=0)
            p_mem = p_mem + jnp.concatenate(rows_mem, axis=0)
            lse_all = jnp.where(lane == head, jnp.concatenate(rows_lse, axis=0), lse_all)
            part = dot_nn(p, mask_half(vp, half))
            total = part if total is None else total + part
        totals.append(total)
    mem_part = dot_nn(p_mem.astype(bf16), stack_heads(v))
    a_ref[...] = (jnp.concatenate(totals, axis=1) + mem_part).astype(bf16)
    lse_acc[0:ROWS] = lse_all

    @pl.when(step == STEPS - 1)
    def _():
        lse_ref[...] = lse_acc[...].T[0:16]


def ffn_fwd_kernel(
    live_ref, tok_ref, mem_ref, a_ref, wo_ref, wu_ref, wd_ref, vec_ref, *refs,
):
    n1_ref, i1_ref, h1b_ref, g_ref, slope_ref, n2_ref, i2_ref, out_ref, next_ref, h1, acc = refs[-11:]
    step = pl.program_id(0)
    live = live_ref[0]

    @pl.when(step == 0)
    def _():
        branch = dot_nn(a_ref[...], wo_ref[...]) + vec_ref[2:3]
        mem = mem_ref[...]
        u = jnp.concatenate([tok_ref[...].astype(f32), mem, mem], axis=0)
        normed, inverse = norm_rows(u + branch)
        n1_ref[...] = normed.astype(bf16)
        i1_ref[...] = inverse
        full = normed * vec_ref[3:4] + vec_ref[4:5]
        h1[...] = full
        h1b_ref[...] = full.astype(bf16)
        acc[...] = full + vec_ref[5:6]

    bias = vec_ref[pl.ds(8 + step, 1), :]
    blocks = [slice(272 * i, 272 * i + 272) for i in range(2)]
    ahead = dot_nt(h1b_ref[blocks[0]], wu_ref[...]) + bias
    for index, rows in enumerate(blocks):
        z = ahead
        if index + 1 < len(blocks):
            ahead = dot_nt(h1b_ref[blocks[index + 1]], wu_ref[...]) + bias
        g, slope = gelu_parts(z)
        g = g.astype(bf16)
        g_ref[rows] = g
        slope_ref[rows] = slope.astype(bf16)
        acc[rows] += dot_nn(g, wd_ref[...])

    @pl.when(step == CHUNKS - 1)
    def _():
        normed, inverse = norm_rows(acc[...])
        n2_ref[...] = normed.astype(bf16)
        i2_ref[...] = inverse
        y = normed * vec_ref[6:7] + vec_ref[7:8]
        row = lax.broadcasted_iota(jnp.int32, (SEG_LEN, 1), 0)
        out_ref[...] = jnp.where(row < live, y[0:SEG_LEN], 0.0)
        next_ref[...] = jnp.where(live > 0, y[SEG_LEN + PADM:ROWS], mem_ref[...])


def ffn_bwd_kernel(
    live_ref, cot_ref, dmem_ref, n1_ref, i1_ref, n2_ref, i2_ref, slope_ref, wo_ref, wu_ref, wd_ref, vec_ref,
    dfb_ref, dzb_ref, dob_ref, dr1_ref, da_ref, sums_ref,
    acc,
):
    step = pl.program_id(0)
    live = live_ref[0]

    @pl.when(step == 0)
    def _():
        row = lax.broadcasted_iota(jnp.int32, (SEG_LEN, 1), 0)
        token = jnp.where(row < live, cot_ref[...].astype(f32), 0.0)
        write = jnp.where(live > 0, dmem_ref[...], 0.0)
        dy = jnp.concatenate([token, jnp.zeros((PADM, D), f32), write], axis=0)
        normed = n2_ref[...].astype(f32)
        sums_ref[...] = jnp.zeros_like(sums_ref)
        sums_ref[6:7] = jnp.sum(dy * normed, axis=0, keepdims=True)
        sums_ref[7:8] = jnp.sum(dy, axis=0, keepdims=True)
        back = norm_back(dy, normed, i2_ref[...], vec_ref[6:7])
        low = back.astype(bf16)
        dfb_ref[...] = low
        sums_ref[5:6] = jnp.sum(low.astype(f32), axis=0, keepdims=True)
        acc[...] = back

    blocks = [slice(ROWS // 2 * i, ROWS // 2 * (i + 1)) for i in range(2)]
    ahead = dot_nt(dfb_ref[blocks[0]], wd_ref[...])
    total = None
    for index, rows in enumerate(blocks):
        dg = ahead
        if index + 1 < len(blocks):
            ahead = dot_nt(dfb_ref[blocks[index + 1]], wd_ref[...])
        dz = (dg * slope_ref[rows].astype(f32)).astype(bf16)
        dzb_ref[rows] = dz
        part = jnp.sum(dz.astype(f32), axis=0, keepdims=True)
        total = part if total is None else total + part
        acc[rows] += dot_nn(dz, wu_ref[...])
    sums_ref[pl.ds(8 + step, 1), :] = total

    @pl.when(step == CHUNKS - 1)
    def _():
        dh = acc[...]
        normed = n1_ref[...].astype(f32)
        sums_ref[3:4] = jnp.sum(dh * normed, axis=0, keepdims=True)
        sums_ref[4:5] = jnp.sum(dh, axis=0, keepdims=True)
        back = norm_back(dh, normed, i1_ref[...], vec_ref[3:4])
        dr1_ref[...] = back
        low = back.astype(bf16)
        dob_ref[...] = low
        sums_ref[2:3] = jnp.sum(low.astype(f32), axis=0, keepdims=True)
        da_ref[...] = dot_nt(low, wo_ref[...]).astype(bf16)


def attn_bwd_kernel(
    first, outs, live_ref, q_ref, k_ref, v_ref, da_ref, lse_ref, dr1_ref, wq_ref, wk_ref, wv_ref, *refs,
):
    dq_ref, dk_ref, dv_ref, sums_ref, du_ref, *token_refs = refs[-outs:]
    live = live_ref[0]
    step = first + pl.program_id(0)

    @pl.when(step == first)
    def _():
        du_ref[...] = dr1_ref[...]

    valid = valid_positions((ROWS, 1), 0, live)
    for pair in range(COLS // 128):
        cols = slice(128 * pair, 128 * pair + 128)
        qp, kp, vp, dap = q_ref[:, cols], k_ref[:, cols], v_ref[:, cols], da_ref[:, cols]
        dq = dk = dv = None
        for half in range(2):
            head = step * (COLS // HEAD) + 2 * pair + half
            kh, vh, qh, dah = (mask_half(t, half) for t in (kp, vp, qp, dap))
            s = dot_nt(kh, qp)
            s = jnp.where(valid, s, neg_large)
            p = jnp.exp2(s * SCORE2 - lse_ref[pl.ds(head, 1), 0:ROWS])
            dp = dot_nt(vh, dap)
            inner = jnp.sum(p * dp, axis=0, keepdims=True)
            ds = (p * (dp - inner)).astype(bf16)
            parts = (dot_tn(ds, kh), dot_nn(ds, qh), dot_nn(p.astype(bf16), dah))
            if dq is None:
                dq, dk, dv = parts
            else:
                dq, dk, dv = dq + parts[0], dk + parts[1], dv + parts[2]
        dq_ref[:, cols] = (dq * ROOT).astype(bf16)
        dk_ref[:, cols] = (dk * ROOT).astype(bf16)
        dv_ref[:, cols] = dv.astype(bf16)
    dq, dk, dv = dq_ref[...], dk_ref[...], dv_ref[...]
    sums_ref[0:1] = jnp.sum(dq.astype(f32), axis=0, keepdims=True)
    sums_ref[1:2] = jnp.sum(dv.astype(f32), axis=0, keepdims=True)
    du_ref[...] += dot_nt(dq, wq_ref[...]) + dot_nt(dk, wk_ref[...]) + dot_nt(dv, wv_ref[...])
    for token_ref in token_refs:
        @pl.when(step == STEPS - 1)
        def _(token_ref=token_ref):
            token_ref[...] = du_ref[0:SEG_LEN]


def grad_kernel(plan, count, bits_ref, *refs):
    keep_ref, other_ref, made, sems = refs[count:]
    step = pl.program_id(0)
    core = bits_ref[BITS.index("c")]
    copies = []
    for index, pairs in enumerate(plan):
        ways = []
        for part in range(8):
            shard, third = divmod(8 * index + part, 3)
            source = made.at[index, pl.ds(96 * part, 96)]
            ways.append([
                pltpu.make_async_copy(source, target.at[shard // 2, pl.ds(96 * third, 96)], sems.at[index, part])
                for target in (keep_ref, other_ref)
            ])
        copies += ways

        @pl.when(step == index)
        def _(pairs=pairs, index=index, ways=ways):
            left = jnp.concatenate([refs[item][...] for item, _ in pairs], axis=0)
            blocks = len(pairs[0][1])
            width = D // blocks
            for block in range(blocks):
                right = jnp.concatenate([refs[items[block]][...] for _, items in pairs], axis=0)
                made[index, :, width * block:width * block + width] = dot_tn(left, right).astype(bf16)
            for part, (keep, other) in enumerate(ways):
                parity = (8 * index + part) // 3 % 2

                @pl.when(core == parity)
                def _(keep=keep):
                    keep.start()

                @pl.when(core != parity)
                def _(other=other):
                    other.start()

    @pl.when(step == len(plan) - 1)
    def _():
        for keep, _ in copies:
            keep.wait()


def spec(shape, index):
    return pl.BlockSpec(shape, index)


def whole(shape):
    return pl.BlockSpec(shape, lambda j: (0,) * len(shape))


SCALAR = pl.BlockSpec(memory_space=pltpu.SMEM)


def shape_of(shape, dtype):
    return jax.ShapeDtypeStruct(shape, dtype)


def params():
    return pltpu.CompilerParams(dimension_semantics=("arbitrary",), vmem_limit_bytes=VMEM_BYTES)


def cost(flops, moved):
    return pl.CostEstimate(flops=int(flops), bytes_accessed=int(moved), transcendentals=0)


def attn_fwd(segment, live, tokens, mem, weights, vectors):
    block = spec((ROWS, COLS), lambda j: (0, j))
    return pl.pallas_call(
        attn_fwd_kernel,
        grid=(STEPS,),
        in_specs=[
            SCALAR, spec((SEG_LEN, D), lambda j: (segment, 0)), whole((PADM, D)),
            spec((D, COLS), lambda j: (0, j)), spec((D, COLS), lambda j: (1, j)), spec((D, COLS), lambda j: (2, j)),
            spec((12, COLS), lambda j: (0, j)),
        ],
        out_specs=[whole((ROWS, D)), block, block, block, whole((16, ROWS_LANES)), block],
        out_shape=[shape_of((ROWS, D), bf16)] * 4 + [shape_of((16, ROWS_LANES), f32), shape_of((ROWS, D), bf16)],
        scratch_shapes=[pltpu.VMEM((ROWS_LANES, 128), f32)],
        compiler_params=params(),
        name="attn_fwd",
        cost_estimate=cost(5e9, 8e6),
    )(live, tokens, mem, weights, weights, weights, vectors)


def ffn_fwd(segment, live, tokens, mem, attended, weights, vectors, output):
    full = whole((ROWS, D))
    chunk = spec((ROWS, D), lambda j: (0, j))
    col = whole((ROWS, 1))
    return pl.pallas_call(
        ffn_fwd_kernel,
        grid=(CHUNKS,),
        in_specs=[
            SCALAR, spec((SEG_LEN, D), lambda j: (segment, 0)), whole((PADM, D)), full,
            spec((D, D), lambda j: (3, 0)), spec((D, D), lambda j: (4 + j, 0)), spec((D, D), lambda j: (8 + j, 0)),
            whole((12, D)),
        ] + [pl.BlockSpec(memory_space=pl.ANY)] * (output is not None),
        out_specs=[full, col, full, chunk, chunk, full, col, spec((SEG_LEN, D), lambda j: (segment, 0)), whole((PADM, D))],
        out_shape=[
            shape_of((ROWS, D), bf16), shape_of((ROWS, 1), f32), shape_of((ROWS, D), bf16), shape_of((ROWS, FF), bf16),
            shape_of((ROWS, FF), bf16), shape_of((ROWS, D), bf16), shape_of((ROWS, 1), f32),
            shape_of((SEGS * SEG_LEN, D), f32), shape_of((PADM, D), f32),
        ],
        input_output_aliases={} if output is None else {8: 7},
        scratch_shapes=[pltpu.VMEM((ROWS, D), f32)] * 2,
        compiler_params=params(),
        name="ffn_fwd",
        cost_estimate=cost(6e9, 25e6),
    )(live, tokens, mem, attended, weights, weights, weights, vectors, *([] if output is None else [output]))


def ffn_bwd(segment, live, cotangent, dmem, saved, weights, vectors):
    n1, i1, h1b, g, slope, n2, i2 = saved
    full = whole((ROWS, D))
    chunk = spec((ROWS, D), lambda j: (0, j))
    col = whole((ROWS, 1))
    return pl.pallas_call(
        ffn_bwd_kernel,
        grid=(CHUNKS,),
        in_specs=[
            SCALAR, spec((SEG_LEN, D), lambda j: (segment, 0)), whole((PADM, D)), full, col, full, col, chunk,
            spec((D, D), lambda j: (3, 0)), spec((D, D), lambda j: (4 + j, 0)), spec((D, D), lambda j: (8 + j, 0)),
            whole((12, D)),
        ],
        out_specs=[full, chunk, full, full, full, whole((12, D))],
        out_shape=[
            shape_of((ROWS, D), bf16), shape_of((ROWS, FF), bf16), shape_of((ROWS, D), bf16),
            shape_of((ROWS, D), f32), shape_of((ROWS, D), bf16), shape_of((12, D), f32),
        ],
        scratch_shapes=[pltpu.VMEM((ROWS, D), f32)],
        compiler_params=params(),
        name="ffn_bwd",
        cost_estimate=cost(6e9, 25e6),
    )(live, cotangent, dmem, n1, i1, n2, i2, slope, weights, weights, weights, vectors)


def attn_bwd(first, steps, segment, token_grad, live, q, k, v, da, lse, du, weights):
    block = spec((ROWS, COLS), lambda j: (0, first + j))
    own = spec((ROWS, COLS), lambda j: (0, j))
    last = first + steps == STEPS
    given = [token_grad] if last and token_grad is not None else []
    return pl.pallas_call(
        functools.partial(attn_bwd_kernel, first, 5 + last),
        grid=(steps,),
        in_specs=[
            SCALAR, block, block, block, block, whole((16, ROWS_LANES)), whole((ROWS, D)),
            spec((D, COLS), lambda j: (0, first + j)), spec((D, COLS), lambda j: (1, first + j)),
            spec((D, COLS), lambda j: (2, first + j)),
        ] + [pl.BlockSpec(memory_space=pl.ANY)] * len(given),
        out_specs=[own, own, own, spec((8, COLS), lambda j: (0, j)), whole((ROWS, D))]
        + [spec((SEG_LEN, D), lambda j: (segment, 0))] * last,
        out_shape=[shape_of((ROWS, steps * COLS), bf16)] * 3 + [
            shape_of((8, steps * COLS), f32), shape_of((ROWS, D), f32)]
        + [shape_of((SEGS * SEG_LEN, D), f32)] * last,
        input_output_aliases={10: 5} if given else {},
        compiler_params=params(),
        name="attn_bwd",
        cost_estimate=cost(4e9, 5e6),
    )(live, q, k, v, da, lse, du, weights, weights, weights, *given)


def grad_piece(products, name):
    arrays, specs, plan = [], [], []

    def add(array, chunk, width):
        for index, (have, *at) in enumerate(arrays):
            if have is array and at == [chunk, width]:
                return index
        arrays.append((array, chunk, width))
        specs.append(spec((ROWS, width), lambda j: (0, chunk)))
        return len(arrays) - 1

    def add_right(right):
        return [add(*part, COLS) for part in right] if isinstance(right, list) else [add(right, 0, D)]

    for lefts, chunk, rights in products:
        plan.append([(add(left, chunk, D), add_right(right)) for left, right in zip(lefts, rights)])
    anywhere = pl.BlockSpec(memory_space=pl.ANY)
    return pl.pallas_call(
        functools.partial(grad_kernel, plan, len(arrays)),
        grid=(len(plan),),
        in_specs=[SCALAR] + specs,
        out_specs=[anywhere] * 2,
        out_shape=[shape_of((4, 288, D), bf16)] * 2,
        scratch_shapes=[pltpu.VMEM((3, D, D), bf16), pltpu.SemaphoreType.DMA((3, 8))],
        compiler_params=params(),
        name=name,
        cost_estimate=cost(4e9, 15e6),
    )(rank_bits(), *[item[0] for item in arrays])


BITS = ("y", "x", "z1", "z0", "c")


def rank_bits():
    place, line = lax.axis_index("dp"), lax.axis_index("fsdp")
    return jnp.stack([place // 2 % 2, place % 2, line // 4 % 2, line // 2 % 2, line % 2]).astype(jnp.int32)


STRIDE = {"y": 16, "x": 8, "z1": 4, "z0": 2, "c": 1}


def swap(value, dims):
    mask = sum(STRIDE[dim] for dim in dims)
    return lax.ppermute(value, ("dp", "fsdp"), [(d, d ^ mask) for d in range(32)])


def add_low(left, right):
    return (left.astype(f32) + right.astype(f32)).astype(bf16)


class Part:
    def __init__(self, keeps, gots, names, dim, split=False):
        self.keeps, self.gots, self.names, self.dim, self.split = keeps, gots, names, dim, split


def columns(items):
    cut = [array[..., block * size:(block + 1) * size] for array, block, size in items]
    return cut[0] if len(cut) == 1 else jnp.concatenate(cut, axis=-1)


def combine(*parts):
    made = []
    for part in parts:
        keep, got = columns(part.keeps), columns(part.gots)
        if part.dim is None:
            made.append(add_low(keep, got))
            continue
        axis = part.names.index(part.dim)
        bit = rank_bits()[BITS.index(part.dim)]
        stays, goes = (
            add_low(*(lax.dynamic_index_in_dim(item, at, axis, keepdims=False) for item in (keep, got)))
            for at in (bit, 1 - bit))
        made.append(stays)
        width = goes.shape[-1] // 2
        made += [goes[..., :width], goes[..., width:]] if part.split else [goes]
    return made


def row_major(array):
    return with_layout_constraint(array, Layout(major_to_minor=tuple(range(array.ndim))))


def exchange(run, values, *sends):
    flat, tree = jax.tree.flatten((values, [array for array, _ in sends]))
    values, arrays = jax.tree.unflatten(tree, lax.optimization_barrier(tuple(flat)))
    arrays = [row_major(array) for array in arrays]
    gots = [row_major(swap(array, (dim,))) for array, (_, dim) in zip(arrays, sends)]
    flat, tree = jax.tree.flatten((run(values), gots))
    result, gots = jax.tree.unflatten(tree, lax.optimization_barrier(tuple(flat)))
    return (result,) + tuple(gots)


def unsplit(pair, parity):
    keep, other = pair
    even, odd = jnp.where(parity == 0, keep, other), jnp.where(parity == 0, other, keep)
    return jnp.stack([even, odd], axis=1).reshape(-1, D)


def column_blocks(parts, index):
    return [(part[index], j) for part in parts for j in range(part[index].shape[1] // COLS)]


def spread(own):
    place = lax.axis_index("dp")
    arrived = []
    for mask, dims in enumerate(((), ("x",), ("y",), ("x", "y"))):
        block = lax.dynamic_index_in_dim(own, place ^ mask, 0, keepdims=False)
        arrived.append(swap(block, dims) if dims else block)
    quarters = jnp.stack(arrived).reshape((2, 2) + arrived[0].shape)
    quarters = jnp.where(place // 2 == 1, quarters[::-1], quarters)
    quarters = jnp.where(place % 2 == 1, quarters[:, ::-1], quarters)
    return quarters.reshape(-1, D).astype(f32)


def adam_update(parameter, gradient, moment_one, moment_two, decay_factor):
    new_one = beta_one * moment_one + (1.0 - beta_one) * gradient
    new_two = beta_two * moment_two + (1.0 - beta_two) * gradient * gradient
    corrected_one = new_one / (1.0 - beta_one**adam_step)
    corrected_two = new_two / (1.0 - beta_two**adam_step)
    update = corrected_one / (jnp.sqrt(corrected_two) + adam_eps) + decay_factor * parameter
    return (update, new_one, new_two)


def local_grads(tokens, memory_init, chain_tokens, cotangent, weights, vectors):
    mem = jnp.pad(memory_init, ((0, PADM - MEM), (0, 0)))
    lives = [jnp.clip(chain_tokens - s * SEG_LEN, 0, SEG_LEN) for s in range(SEGS)]
    kept = []
    out = None
    for s in range(SEGS):
        x, q, k, v, lse, a = attn_fwd(s, lives[s], tokens, mem, weights, vectors)
        *saved, out, mem = ffn_fwd(s, lives[s], tokens, mem, a, weights, vectors, out)
        kept.append((x, q, k, v, lse, a, saved))
    dmem = jnp.zeros((PADM, D), f32)
    back = [None] * SEGS
    token_grad = None
    pick = lambda items, i: [item[i] for item in items]
    x, a = pick(kept, 0), pick(kept, 5)
    h, g = ([k_[6][i] for k_ in kept] for i in (2, 3))
    custom = (lax.axis_size("dp"), lax.axis_size("fsdp")) == (4, 8)
    custom = (lax.axis_size("dp"), lax.axis_size("fsdp")) == (4, 8)
    for s in reversed(range(SEGS)):
        _, q, k, v, lse, _, saved = kept[s]
        dfb, dzb, dob, du, da, sums = ffn_bwd(s, lives[s], cotangent, dmem, saved, weights, vectors)
        back[s] = (dfb, dzb, dob, sums)
        parts = []

        def attend(state, steps=1, s=s, parts=parts):
            *part, sums_qv, out = (made := attn_bwd(
                len(parts), steps, s, state[3], lives[s], *kept[s][1:4], *state[:3], weights))[:5]
            parts.append((*part, sums_qv))
            return (state[0], state[1], out, made[5] if len(made) > 5 else state[3])

        state = (da, lse, du, token_grad)
        if s > 0:
            state = attend(state, STEPS)
            back[s] += (parts,)
        else:
            df, dz, do = (pick(back, i) for i in range(3))
            run_down = lambda df: grad_piece([(g, 1, df), (g, 2, df), (g, 3, df)], "grad_down")
            run_mixed = lambda dz: grad_piece([(dz, 2, h), (dz, 3, h), (g, 0, df)], "grad_mixed")
            run_up = lambda do: grad_piece([(a, 0, do), (dz, 0, h), (dz, 1, h)], "grad_up")
            back[0] += (parts,)
            run_qkv = lambda x: grad_piece(
                [(x, 0, [column_blocks(item[4], i) for item in back]) for i in range(3)], "grad_qkv")
            down = run_down(df)
            if not custom:
                mixed, up = run_mixed(dz), run_up(do)
                for _ in range(STEPS):
                    state = attend(state)
            else:
                full = lambda *items: [(item, 0, item.shape[-1]) for item in items]
                view = lambda item: item.reshape((2,) * 4 + (72, D))
                plane = ["z1", "z0", "y", "x"]
                d_keep, d_send = map(view, down)
                mixed, d_got = exchange(run_mixed, dz, (d_send, "c"))
                d_keep, d_left, d_right = combine(Part(full(d_keep), full(d_got), plane, "x", True))
                m_keep, m_send = map(view, mixed)
                up, d_got, m_got = exchange(run_up, do, (d_left, "x"), (m_send, "c"))
                m_keep, m_left, m_right = combine(Part(full(m_keep), full(m_got), plane, "z0", True))
                u_keep, u_send = map(view, up)
                state, d_more, m_got, u_got = exchange(attend, state, (d_right, "x"), (m_left, "z0"), (u_send, "c"))
                d_keep, d_send, u_keep, u_left, u_right = combine(
                    Part(full(d_keep), full(d_got, d_more), ["z1", "z0", "y"], "y"),
                    Part(full(u_keep), full(u_got), plane, "x", True))
                state, d_got, m_more, u_got = exchange(attend, state, (d_send, "y"), (m_right, "z0"), (u_left, "x"))
                d_keep, d_send, m_keep, m_send = combine(
                    Part(full(d_keep), full(d_got), ["z1", "z0"], "z0"),
                    Part(full(m_keep), full(m_got, m_more), ["z1", "y", "x"], "y"))
                state, d_got, m_got, u_more = exchange(attend, state, (d_send, "z0"), (m_send, "y"), (u_right, "x"))
                d_keep, d_send, m_keep, m_send, u_keep, u_send = combine(
                    Part(full(d_keep), full(d_got), ["z1"], "z1"),
                    Part(full(m_keep), full(m_got), ["z1", "x"], "x"),
                    Part(full(u_keep), full(u_got, u_more), ["z1", "z0", "y"], "y"))
        du, token_grad = state[2:]
        dmem = du[SEG_LEN:SEG_LEN + PADM] + du[SEG_LEN + PADM:] + jnp.where(lives[s] > 0, 0.0, dmem)
    sums = sum(pick(back, 3))
    sums_qv = sum(jnp.concatenate([part[3] for part in item[4]], axis=1) for item in back)
    small = jnp.concatenate([sums_qv[0:2], sums[2:], dmem[:MEM]], axis=0)
    if custom:
        plus = lambda dim: (lambda value: value + swap(value, (dim,)))
        (triple, small), d_got, m_got, u_got = exchange(
            lambda both: (run_qkv(both[0]), plus("c")(both[1])), (x, small),
            (d_send, "z1"), (m_send, "x"), (u_send, "y"))
        m_keep, m_send, u_keep, u_send = combine(
            Part(full(m_keep), full(m_got), ["z1"], "z1"), Part(full(u_keep), full(u_got), ["z1", "z0"], "z0"))
        t_keep, t_send = map(view, triple)
        small, t_got = exchange(plus("z0"), small, (t_send, "c"))
        halves = lambda item: [[(item, i, D // 2)] for i in range(2)]
        (k0, k1), (g0, g1) = halves(t_keep), halves(t_got)
        k0, s0, k1, s1 = combine(Part(k0, g0, plane, "x"), Part(k1, g1, plane, "y"))
        small, g0, g1, u_got = exchange(plus("z1"), small, (s0, "x"), (s1, "y"), (u_send, "z0"))
        k0, s0, k1, s1, u_keep, u_send = combine(
            Part(full(k0), full(g0), ["z1", "z0", "y"], "y"), Part(full(k1), full(g1), ["z1", "z0", "x"], "x"),
            Part(full(u_keep), full(u_got), ["z1"], "z1"))
        _, g0, g1, u_got = exchange(lambda value: value, (), (s0, "y"), (s1, "x"), (u_send, "z1"))
        t_keep, t_send = combine(Part(full(k0, k1), full(g0, g1), ["z1", "z0"], "z0"))
        small, t_got, m_got = exchange(plus("x"), small, (t_send, "z0"), (m_send, "z1"))
        t_keep, t_send = combine(Part(full(t_keep), full(t_got), ["z1"], "z1"))
        small, t_got = exchange(plus("y"), small, (t_send, "z1"))
        own = combine(*(Part(full(k), full(g), [], None) for k, g in (
            (t_keep, t_got), (u_keep, u_got), (m_keep, m_got), (d_keep, d_got))))
        weight_sum = spread(jnp.stack(own))
    else:
        parity = lax.axis_index("fsdp") % 2
        total = jnp.concatenate([unsplit(item, parity) for item in (run_qkv(x), up, mixed, down)], axis=0)
        weight_sum = lax.psum_scatter(total, ("dp", "fsdp"), scatter_dimension=0, tiled=True).astype(f32)
        small = lax.psum(small, ("dp", "fsdp"))
    return (out, token_grad, weight_sum, small)


def shards(
    tokens, memory_init, chain_tokens, cotangent, weights, weight_first, weight_second,
    vectors, vector_first, vector_second,
):
    axes = ("dp", "fsdp")
    total_chains = tokens.shape[0] * lax.axis_size(axes)
    grad_scale = float(total_chains * SEGS * SEG_LEN) ** (-0.5)
    gathered = lax.all_gather(weights.astype(bf16), axes, axis=0, tiled=True)
    output, token_grad, weight_sum, small = local_grads(
        tokens[0], memory_init, chain_tokens, cotangent[0], gathered, vectors)
    vector_sum, memory_sum = small[:-MEM], small[-MEM:]
    weight_grad = weight_sum * grad_scale
    vector_grad = vector_sum * grad_scale
    memory_grad = memory_sum * grad_scale
    weight_step, new_weight_first, new_weight_second = adam_update(
        weights, weight_grad, weight_first, weight_second, decay_rate)
    vector_step, new_vector_first, new_vector_second = adam_update(
        vectors, vector_grad, vector_first, vector_second, 0.0)
    return (
        output[None], token_grad[None], memory_grad, weight_grad, weight_step, new_weight_first, new_weight_second,
        vector_grad, vector_step, new_vector_first, new_vector_second,
    )


def solution(mesh):
    both = ("dp", "fsdp")
    chain = P(both, None, None)
    rows = P(both, None)
    return jax.shard_map(
        shards,
        mesh=mesh,
        in_specs=(chain, P(), P(both), chain, rows, rows, rows, P(), P(), P()),
        out_specs=(chain, chain, P(), rows, rows, rows, rows, P(), P(), P(), P()),
        check_vma=False,
    )
```
